256 devices in a mesh: dp: 64 (over y_lo, x, z), mp: 4 (over y_hi, core).
Axes of the slice: x: 4, y: 4 (y_hi: 2, y_lo: 2; y = y_hi * 2 + y_lo), z: 8, core: 2. Of those that a mesh axis runs over, the one named last changes fastest.
Arguments:
- mixer_vectors: bfloat16 [98304, 4096], P('dp', 'mp'), may hold values from -16 to 16
- upstream_adjoint: bfloat16 [98304, 2, 1792], P('dp', None, 'mp'), may hold values from -6 to 6
- relative_benefit: float32 [98304], P('dp'), may hold values from -4 to 4
- present_policy_logit: float32 [98304], P('dp'), may hold values from -1.5 to 0
- behaviour_policy_logit: float32 [98304], P('dp'), may hold values from -1.5 to 0
- retained_entries: int32 [64, 768], P('dp'), may hold values from 0 to 1535, as said below
- tallies: int32 [64], P('dp'), may hold values from 1 to 768, as said below
- keeper_slot: int32 [32], replicated, may hold values from 0 to 31, each once
Outputs:
- update: bfloat16 [64, 128, 1792], P('dp', None, 'mp')
- gradient: float32 [64, 128, 1792], P('dp', None, 'mp')
The draws below stay inside these ranges and needn't reach their ends.
Inputs may be any that keep to these rules, and one draw needn't show every extreme that they name: `retained_entries`: the 768 slots of one shard name distinct rows of that shard. `tallies`: some shard has all 768 slots live. `keeper_slot`: every owner slot is taken by one head.
All inputs are finite; a program needn't handle non-finite values.
Results may differ from the reference program's by a relative error of at most 0.0046.
The reference program's roundings to bfloat16 on the way (of `scaled`) count: a program that leaves them out, or rounds other values in their place, can miss the bound.
Values may be sent and summed in bfloat16 or wider, within the bound.
No kernel may reach another device: no remote copies, remote signals or barrier semaphores. Data moves between devices by JAX's collectives and lax.ppermute only.
A program may use at most 192 MiB of HBM per device.

```python
import math
import jax
import jax.numpy as jnp
from jax import lax

HEADS = 32
HD = 128
SAMPLES_OF_GROUP = 1536
DHALF = 1792
CAP = 768
SHARDS = 64
TOKENS = 98304


def draw_retained_entries(key, part):
    key = jax.random.fold_in(key, 11)
    key_list = jax.random.split(key, SHARDS)

    def draw_row(row_key):
        return jax.random.permutation(row_key, SAMPLES_OF_GROUP)[:CAP]
    chosen = jax.vmap(draw_row)(key_list)
    return chosen.astype(jnp.int32)


def draw_tallies(key, part):
    key = jax.random.fold_in(key, 23)
    key_one, key_two = jax.random.split(key)
    distribute_rows = jax.random.randint(key_one, (SHARDS,), 1, CAP + 1)
    fullest = jax.random.randint(key_two, (), 0, SHARDS)
    return jnp.where(jnp.arange(SHARDS) == fullest, CAP, distribute_rows).astype(jnp.int32)


def raised(result, rng, source, target, blocks, factor):
    def block_of(position):
        return (jnp.arange(result.shape[position]) // (result.shape[position] // blocks)).reshape((-1,) + (1,) * (result.ndim - 1 - position))

    first = jax.random.permutation(rng, blocks)[block_of(target)]
    far = (block_of(target) + blocks // 2) % blocks
    return jnp.where((block_of(source) == first) | (block_of(source) == far), factor * result, result)


def level_of(own_key, dims, pieces, least, largest):
    loudness, own = 1.0, jax.random.fold_in(own_key, 6)
    for dim, shards_of in pieces:
        steps = jnp.exp(jax.random.uniform(jax.random.fold_in(own, dim), (shards_of,), jnp.float32, least / len(pieces), largest / len(pieces)))
        loudness = loudness * jnp.repeat(steps, dims[dim] // shards_of).reshape([-1 if axis == dim else 1 for axis in range(len(dims))])
    return loudness


def scatter_about(own_key, shape, spread, reach, pieces=(), kind=jnp.bfloat16):
    gain = level_of(own_key, shape, pieces, -0.22, 0.18) if pieces else 1.0
    entries = jax.random.normal(own_key, shape, jnp.float32) * spread * gain
    return jnp.minimum(jnp.maximum(entries, -reach), reach).astype(kind)


def gaussian_with(key, extent, scale, reach, cuts, heavy, kind=jnp.bfloat16):
    values = scale * jax.random.normal(key, extent, jnp.float32)
    if cuts:
        values = values * level_of(key, extent, cuts, -0.22, 0.18)
    return jnp.clip(raised(values, jax.random.fold_in(key, 3), *heavy), -reach, reach).astype(kind)


def setup_inputs(seed: int = 0) -> dict:
    arg_keys = jax.random.split(jax.random.key(seed), 9)
    mixer_vectors = gaussian_with(arg_keys[0], (TOKENS, HEADS * HD), 1.0, 16.0, ((0, 64), (1, 4)), (0, 1, 64, 4.0))
    upstream_adjoint = scatter_about(arg_keys[1], (TOKENS, 2, DHALF), 1.0, 6.0, ((0, 64), (2, 4)))
    relative_benefit = scatter_about(arg_keys[2], (TOKENS,), 1.0, 4.0, ((0, 64),), jnp.float32)
    present_policy_logit = jnp.clip(-1.5 + 1.5 * jax.random.uniform(arg_keys[3], (TOKENS,), jnp.float32) ** level_of(arg_keys[3], (TOKENS,), ((0, 64),), -0.2, 0.2), -1.5, 0.0)
    behaviour_policy_logit = jnp.clip(-1.5 + 1.5 * jax.random.uniform(arg_keys[4], (TOKENS,), jnp.float32) ** level_of(arg_keys[4], (TOKENS,), ((0, 64),), -0.2, 0.2), -1.5, 0.0)
    retained_entries = draw_retained_entries(jax.random.fold_in(arg_keys[8], 71), 0)
    tallies = draw_tallies(jax.random.fold_in(arg_keys[8], 71), 0)
    keeper_slot = jax.random.permutation(arg_keys[7], HEADS).astype(jnp.int32)
    return {"mixer_vectors": mixer_vectors, "upstream_adjoint": upstream_adjoint, "relative_benefit": relative_benefit, "present_policy_logit": present_policy_logit, "behaviour_policy_logit": behaviour_policy_logit, "retained_entries": retained_entries, "tallies": tallies, "keeper_slot": keeper_slot}


coeff_a = 3.4445
coeff_b = -4.775
coeff_c = 2.0315
norm_eps = 1e-06

def orthogonalize(gradient_block):
    highest_precision_mode = lax.Precision.HIGHEST
    norm_scale = jnp.sqrt(jnp.sum(gradient_block * gradient_block)) + norm_eps
    iterate = gradient_block / norm_scale
    for sweep in range(2):
        gram_sum = jnp.dot(iterate, iterate.T, precision=highest_precision_mode)
        poly_mix = coeff_b * gram_sum + coeff_c * jnp.dot(gram_sum, gram_sum, precision=highest_precision_mode)
        iterate = coeff_a * iterate + jnp.dot(poly_mix, iterate, precision=highest_precision_mode)
    return (0.2 * math.sqrt(2 * DHALF) * iterate).astype(jnp.bfloat16)

def reference(mixer_vectors, upstream_adjoint, relative_benefit, present_policy_logit, behaviour_policy_logit, retained_entries, tallies, keeper_slot):
    full_width = 2 * DHALF

    def accumulate(running, group_number):
        kept_samples = retained_entries[group_number] + group_number * SAMPLES_OF_GROUP
        active = jnp.arange(CAP, dtype=jnp.int32) < tallies[group_number]
        weight = jnp.where(active, relative_benefit[kept_samples] * jnp.exp(present_policy_logit[kept_samples] - behaviour_policy_logit[kept_samples]), 0.0)
        scaled = (weight[:, None, None] * upstream_adjoint[kept_samples].astype(jnp.float32)).astype(jnp.bfloat16)
        values = mixer_vectors[kept_samples]
        product = jnp.dot(values.T, scaled.reshape(CAP, full_width), preferred_element_type=jnp.float32)
        return (running + product, None)
    running = lax.scan(accumulate, jnp.zeros((HEADS * HD, full_width), jnp.float32), jnp.arange(SHARDS, dtype=jnp.int32))[0]
    blocks = running.reshape(HEADS, HD, full_width)
    updates = lax.map(orthogonalize, blocks)
    update = updates.reshape(HEADS, HD, 2, DHALF).transpose(2, 0, 1, 3).reshape(2 * HEADS, HD, DHALF)
    holder_grads = blocks.reshape(HEADS, HD, 2, DHALF).transpose(2, 0, 1, 3)
    owner_blocks = jnp.zeros_like(holder_grads).at[:, keeper_slot].set(holder_grads)
    return (update, owner_blocks.reshape(2 * HEADS, HD, DHALF))
```

```python
import math

import jax
import jax.numpy as jnp
import numpy as np
from jax import lax
from jax.experimental import pallas as pl
from jax.experimental.pallas import tpu as pltpu
from jax.sharding import Mesh
from jax.sharding import PartitionSpec as P

DHALF = 1792

coeff_a = 3.4445
coeff_b = -4.775
coeff_c = 2.0315
norm_eps = 1e-06
highest_precision_mode = lax.Precision.HIGHEST

YL, X, Z, YH, C = 2, 4, 8, 2, 2
NAMES = ("yl", "x", "z", "yh", "c")
VIA_PARTNER = 256


def ring_pairs(flip):
    def index(y):
        return (y % 2) * 2 + y // 2

    return [(index(y), index(y ^ flip)) for y in range(4)]


def over_y(value, flip):
    return lax.ppermute(value, ("yl", "yh"), ring_pairs(flip))


def shift(value, axis, size, step):
    return lax.ppermute(value, axis, [(i, (i + step) % size) for i in range(size)])


def odd_to_even(value, step):
    pairs = [
        (x * 2 + c, (x + step) % X * 2 + c) for x in range(X) for c in range(C) if (x + c) % 2
    ]
    return lax.ppermute(value, ("x", "c"), pairs)


def even_to_odd_core(value):
    pairs = [(x * 2 + c, x * 2 + 1 - c) for x in range(X) for c in range(C) if not (x + c) % 2]
    return lax.ppermute(value, ("x", "c"), pairs)


def partial_kernel(plan, s_ref, own_ref, e1_ref, oa_ref, ob_ref, e3_ref, *out_refs):
    cap = own_ref.shape[0]
    first = oa_ref.shape[0]
    for slot, out_ref in enumerate(out_refs):
        chunk, side = plan[slot], plan[4 + slot]

        def term(lo, hi, v_ref, side=side):
            return jnp.dot(s_ref[side, :, lo:hi], v_ref[...], preferred_element_type=jnp.float32)

        @pl.when(chunk == 0)
        def _(out_ref=out_ref, term=term):
            out_ref[...] = (term(0, cap, own_ref) + term(cap, 2 * cap, e1_ref)).astype(
                out_ref.dtype
            )

        @pl.when(chunk == 1)
        def _(out_ref=out_ref, term=term):
            out_ref[...] = (
                term(0, first, oa_ref)
                + term(first, cap, ob_ref)
                + term(cap, 2 * cap, e3_ref)
            ).astype(out_ref.dtype)


def partials(plan, s_all, own, e1, oa, ob, e3):
    cap, cols = own.shape
    q = s_all.shape[1]
    tile = 256

    def v_spec(v):
        return pl.BlockSpec((v.shape[0], tile), lambda i, plan: (0, i))

    return pl.pallas_call(
        partial_kernel,
        grid_spec=pltpu.PrefetchScalarGridSpec(
            num_scalar_prefetch=1,
            grid=(cols // tile,),
            in_specs=[pl.BlockSpec(s_all.shape, lambda i, plan: (0, 0, 0))]
            + [v_spec(v) for v in (own, e1, oa, ob, e3)],
            out_specs=[pl.BlockSpec((q, tile), lambda i, plan: (0, i))] * 4,
        ),
        out_shape=[jax.ShapeDtypeStruct((q, cols), jnp.bfloat16)] * 4,
        compiler_params=pltpu.CompilerParams(vmem_limit_bytes=40 * 2**20),
        cost_estimate=pl.CostEstimate(
            flops=8 * q * 2 * cap * cols, bytes_accessed=12 * 2**20, transcendentals=0
        ),
    )(plan, s_all, own, e1, oa, ob, e3)


def polar_kernel(scale, g_ref, *refs):
    out_ref = refs[-1]
    gram = refs[0][...]
    for ref in refs[1:-1]:
        gram = gram + ref[...]

    def mul(a, b):
        return jnp.dot(a, b, precision=highest_precision_mode, preferred_element_type=jnp.float32)

    n = gram.shape[0]
    eye = (
        lax.broadcasted_iota(jnp.int32, (n, n), 0) == lax.broadcasted_iota(jnp.int32, (n, n), 1)
    ).astype(jnp.float32)
    norm = jnp.sqrt(jnp.sum(gram * eye, keepdims=True)) + norm_eps
    a1 = gram / norm / norm
    p1 = coeff_a * eye + coeff_b * a1 + coeff_c * mul(a1, a1)
    a2 = mul(mul(p1, a1), p1)
    p2 = coeff_a * eye + coeff_b * a2 + coeff_c * mul(a2, a2)
    mix = mul(p2, p1) * (scale / norm)
    out_ref[...] = lax.dot_general(
        mix,
        g_ref[...],
        (((1,), (1,)), ((), ())),
        precision=highest_precision_mode,
        preferred_element_type=jnp.float32,
    ).astype(out_ref.dtype)


def polar(g, grams):
    q, n = g.shape
    return pl.pallas_call(
        lambda *refs: polar_kernel(0.2 * math.sqrt(2 * DHALF), *refs),
        out_shape=jax.ShapeDtypeStruct((n, q), jnp.bfloat16),
        compiler_params=pltpu.CompilerParams(vmem_limit_bytes=16 * 2**20),
    )(g, *grams)


def on_device(
    mixer_vectors,
    upstream_adjoint,
    relative_benefit,
    present_policy_logit,
    behaviour_policy_logit,
    retained_entries,
    tallies,
    keeper_slot,
):
    bf16, f32 = jnp.bfloat16, jnp.float32
    yl, x, z = lax.axis_index("yl"), lax.axis_index("x"), lax.axis_index("z")
    yh, core = lax.axis_index("yh"), lax.axis_index("c")
    kept = retained_entries[0]
    cap = kept.shape[0]
    rows = mixer_vectors.shape[0]
    q = upstream_adjoint.shape[2]

    own = mixer_vectors.at[kept].get(mode="promise_in_bounds")
    e3 = over_y(own, 3)
    e1 = over_y(own, 1)
    oa = over_y(e3[:VIA_PARTNER], 1)
    ob = over_y(e1[VIA_PARTNER:], 3)

    pick = lax.broadcasted_iota(jnp.int32, (rows, cap), 0) == kept[None, :]
    weight_all = relative_benefit * jnp.exp(present_policy_logit - behaviour_policy_logit)
    weight = jnp.sum(jnp.where(pick, weight_all[:, None], 0.0), axis=0)
    weight = jnp.where(jnp.arange(cap, dtype=jnp.int32) < tallies[0], weight, 0.0)
    adjoint = upstream_adjoint.transpose(1, 2, 0).reshape(2 * q, rows)
    picked = jnp.dot(adjoint, pick.astype(bf16), preferred_element_type=f32)
    scaled = (weight[None, :] * picked).astype(bf16).reshape(2, q, cap)
    s_keep = lax.dynamic_index_in_dim(scaled, yl, 0, keepdims=False)
    s_send = lax.dynamic_index_in_dim(scaled, 1 - yl, 0, keepdims=False)
    s_own = jnp.concatenate([s_keep, over_y(s_send, 1)], axis=1)
    s_all = jnp.stack([s_own, shift(s_own, "c", C, 1)])

    odd = (x + core) % 2
    near = jnp.where((x + odd) % X // 2 == yh, 0, 1)
    far = 1 - near
    chunk = jnp.where(
        odd == 1, jnp.stack([near, far, near, far]), jnp.stack([far, far, near, near])
    )
    side = jnp.where(odd == 1, jnp.array([1, 0, 0, 1]), jnp.array([0, 1, 1, 0]))
    plan = jnp.concatenate([chunk, side]).astype(jnp.int32)
    t0, t1, t2, t3 = partials(plan, s_all, own, e1, oa, ob, e3)
    ra = shift(t0, "x", X, 1)
    rb = shift(t1, "x", X, -1)
    u2 = t2.astype(f32) + ra.astype(f32)
    u3 = t3.astype(f32) + rb.astype(f32)
    rp = odd_to_even(u2.astype(bf16), 1)
    rm = odd_to_even(u3.astype(bf16), -1)
    keep = (u3 + rp.astype(f32)).astype(bf16)
    cross = even_to_odd_core((u2 + rm.astype(f32)).astype(bf16))
    mine = jnp.where(odd == 1, cross, keep)

    head = mine.shape[1] // Z

    def block(step):
        return lax.dynamic_slice_in_dim(mine, (z + step) % Z * head, head, 1)

    g = block(0).astype(f32)
    for got in [shift(block(d), "z", Z, d) for d in (4, 3, 5, 2, 6, 1, 7)]:
        g = g + got.astype(f32)

    gram = lax.dot_general(
        g, g, (((0,), (0,)), ((), ())), precision=highest_precision_mode,
        preferred_element_type=f32,
    )
    grams = [gram] + [
        lax.ppermute(gram, ("yl", "yh", "c"), [(i, i ^ d) for i in range(8)]) for d in range(1, 8)
    ]
    update = polar(g, grams)

    heads_total = keeper_slot.shape[0]
    heads = jnp.arange(heads_total, dtype=jnp.int32)
    wanted = x * Z + jnp.arange(Z, dtype=jnp.int32)
    source = jnp.sum(
        jnp.where(keeper_slot[None, :] == wanted[:, None], heads[None, :], 0), axis=1
    )
    place = (x - source // Z) % X * Z + source % Z
    spread = lax.all_to_all(g.astype(bf16).reshape(Z, q // Z, head), "z", 0, 0, tiled=True)
    everyone = jnp.concatenate([spread] + [shift(spread, "x", X, d) for d in (1, 2, 3)])
    chosen = everyone.at[place].get(mode="promise_in_bounds")
    arrived = lax.all_to_all(chosen, "z", 0, 0, tiled=True).reshape(q, head)
    gradient = arrived.astype(f32).T
    return (update[None], gradient[None])


def solution(mesh):
    wide = Mesh(np.asarray(mesh.devices).reshape(YL, X, Z, YH, C), NAMES)
    dp, mp = ("yl", "x", "z"), ("yh", "c")
    return jax.shard_map(
        on_device,
        mesh=wide,
        in_specs=(
            P(dp, mp),
            P(dp, None, mp),
            P(dp),
            P(dp),
            P(dp),
            P(dp, None),
            P(dp),
            P(),
        ),
        out_specs=(P(dp, None, mp), P(dp, None, mp)),
        check_vma=False,
    )
```

```python
import math

import jax
import jax.numpy as jnp
import numpy as np
from jax import lax
from jax.experimental import pallas as pl
from jax.experimental.pallas import tpu as pltpu
from jax.sharding import Mesh
from jax.sharding import PartitionSpec as P

DHALF = 1792

coeff_a = 3.4445
coeff_b = -4.775
coeff_c = 2.0315
norm_eps = 1e-06
highest_precision_mode = lax.Precision.HIGHEST

YL, X, Z, YH, C = 2, 4, 8, 2, 2
NAMES = ("yl", "x", "z", "yh", "c")
PIECES = 2


def ring_pairs(flip):
    def index(y):
        return (y % 2) * 2 + y // 2

    return [(index(y), index(y ^ flip)) for y in range(4)]


def over_y(value, flip):
    return lax.ppermute(value, ("yl", "yh"), ring_pairs(flip))


def shift(value, axis, size, step):
    return lax.ppermute(value, axis, [(i, (i + step) % size) for i in range(size)])


def odd_to_even(value, step):
    pairs = [
        (x * 2 + c, (x + step) % X * 2 + c) for x in range(X) for c in range(C) if (x + c) % 2
    ]
    return lax.ppermute(value, ("x", "c"), pairs)


def even_to_odd_core(value):
    pairs = [(x * 2 + c, x * 2 + 1 - c) for x in range(X) for c in range(C) if not (x + c) % 2]
    return lax.ppermute(value, ("x", "c"), pairs)


def pick_kernel(kept_ref, v_ref, out_ref):
    rows, cap = v_ref.shape[0], kept_ref.shape[1]
    column = jnp.broadcast_to(kept_ref[...], (8, cap)).T[:, :1]
    pick = lax.broadcasted_iota(jnp.int32, (cap, rows), 1) == column
    out_ref[...] = jnp.dot(
        pick.astype(jnp.bfloat16), v_ref[...], preferred_element_type=jnp.float32
    ).astype(out_ref.dtype)


def pick_rows(kept, values, piece, pieces):
    rows, cols = values.shape
    cap = kept.shape[1]
    width = cols // pieces
    return pl.pallas_call(
        pick_kernel,
        grid=(1,),
        in_specs=[
            pl.BlockSpec((1, cap), lambda i: (0, 0)),
            pl.BlockSpec((rows, width), lambda i: (0, piece)),
        ],
        out_specs=pl.BlockSpec((cap, width), lambda i: (0, 0)),
        out_shape=jax.ShapeDtypeStruct((cap, width), values.dtype),
        compiler_params=pltpu.CompilerParams(vmem_limit_bytes=32 * 2**20),
        cost_estimate=pl.CostEstimate(
            flops=2 * cap * rows * width, bytes_accessed=2 * (rows + cap) * width, transcendentals=0
        ),
    )(kept, values)


def scale_kernel(plan, kept_ref, benefit_ref, present_ref, behaviour_ref, u_ref, out_ref):
    rows, cap = u_ref.shape[2], kept_ref.shape[1]
    pick = (lax.broadcasted_iota(jnp.int32, (rows, cap), 0) == kept_ref[...]).astype(jnp.bfloat16)
    rest = benefit_ref[...] * jnp.exp(present_ref[...] - behaviour_ref[...])
    parts = []
    for _ in range(3):
        part = rest.astype(jnp.bfloat16)
        parts.append(part)
        rest = rest - part.astype(jnp.float32)
    weight = jnp.zeros((1, cap), jnp.float32)
    for part in parts[::-1]:
        stacked = jnp.broadcast_to(part, (16, rows))
        weight = weight + jnp.dot(stacked, pick, preferred_element_type=jnp.float32)[:1]
    live = lax.broadcasted_iota(jnp.int32, (1, cap), 1) < plan[1]
    weight = jnp.where(live, weight, 0.0)
    picked = jnp.dot(u_ref[0], pick, preferred_element_type=jnp.float32)
    out_ref[...] = (weight * picked).astype(out_ref.dtype)


def scaled_half(half, tally, kept, benefit, present, behaviour, adjoint):
    _, q, rows = adjoint.shape
    cap = kept.shape[1]
    row_spec = pl.BlockSpec((1, rows), lambda i, plan: (0, 0))
    return pl.pallas_call(
        scale_kernel,
        grid_spec=pltpu.PrefetchScalarGridSpec(
            num_scalar_prefetch=1,
            grid=(1,),
            in_specs=[
                pl.BlockSpec((1, cap), lambda i, plan: (0, 0)),
                row_spec,
                row_spec,
                row_spec,
                pl.BlockSpec((1, q, rows), lambda i, plan: (plan[0], 0, 0)),
            ],
            out_specs=pl.BlockSpec((q, cap), lambda i, plan: (0, 0)),
        ),
        out_shape=jax.ShapeDtypeStruct((q, cap), jnp.bfloat16),
        compiler_params=pltpu.CompilerParams(vmem_limit_bytes=32 * 2**20),
        cost_estimate=pl.CostEstimate(
            flops=2 * q * rows * cap, bytes_accessed=2 * q * (rows + cap), transcendentals=rows
        ),
    )(jnp.stack([half, tally]).astype(jnp.int32), kept, benefit, present, behaviour, adjoint)


def partial_kernel(parts, plan, *refs):
    s_refs, v_refs, out_refs = refs[:4], refs[4:-6], refs[-6:-2]
    s_all, total = refs[-2:]
    own_ref, e1_ref, e3_ref = v_refs[:3]
    opposite = v_refs[3:]
    q, cap = s_refs[0].shape
    tile = total.shape[2]
    for i, ref in enumerate(s_refs):
        side, other = divmod(i, 2)
        s_all[side * q : (side + 1) * q, other * cap : (other + 1) * cap] = ref[...]

    for tile_at in range(0, own_ref.shape[1], tile):
        columns = slice(tile_at, tile_at + tile)

        def dot(lo, v, columns=columns):
            return jnp.dot(
                s_all[:, lo : lo + v.shape[0]], v[:, columns], preferred_element_type=jnp.float32
            )

        near = dot(cap, e1_ref) + dot(0, own_ref)
        far = dot(cap, e3_ref)
        at = 0
        for ref in opposite:
            far = far + dot(at, ref)
            at += ref.shape[0]
        for chunk, value in enumerate((near, far)):
            value = value.astype(total.dtype)
            for side in range(2):
                total[2 * chunk + side] = value[side * q : (side + 1) * q]
        for slot, out_ref in enumerate(out_refs):
            out_ref[:, columns] = total[plan[slot]]


def partials(plan, s_list, own, e1, e3, opposite):
    cap, cols = own.shape
    q = s_list[0].shape[0]
    values = [own, e1, e3, *opposite]
    full = pl.BlockSpec(memory_space=pltpu.VMEM)
    return pl.pallas_call(
        lambda *refs: partial_kernel(len(opposite), *refs),
        in_specs=[pl.BlockSpec(memory_space=pltpu.SMEM)] + [full] * (4 + len(values)),
        out_specs=[full] * 4,
        scratch_shapes=[
            pltpu.VMEM((2 * q, 2 * cap), jnp.bfloat16),
            pltpu.VMEM((4, q, 256), jnp.bfloat16),
        ],
        out_shape=[jax.ShapeDtypeStruct((q, cols), jnp.bfloat16)] * 4,
        compiler_params=pltpu.CompilerParams(vmem_limit_bytes=40 * 2**20),
        cost_estimate=pl.CostEstimate(
            flops=8 * q * 2 * cap * cols, bytes_accessed=8 * 2**20, transcendentals=0
        ),
    )(plan, *s_list, *values)


def rows_kernel(piece_count, plan, *refs):
    ins, outs, mine = refs[: 4 * piece_count], refs[4 * piece_count : -1], refs[-1]
    width = ins[0].shape[1]
    rows = outs[0].shape[0]
    for piece in range(piece_count):
        cross, t3, rb, rp = ins[4 * piece : 4 * piece + 4]
        columns = pl.ds(piece * width, width)

        @pl.when(plan[0] == 1)
        def _(cross=cross, columns=columns):
            mine[:, columns] = cross[...].astype(jnp.float32)

        @pl.when(plan[0] == 0)
        def _(t3=t3, rb=rb, rp=rp, columns=columns):
            mine[:, columns] = (
                t3[...].astype(jnp.float32)
                + rb[...].astype(jnp.float32)
                + rp[...].astype(jnp.float32)
            )

    for step, out in enumerate(outs):
        at = lax.rem(plan[1] + step, Z) * rows
        out[...] = mine[pl.ds(pl.multiple_of(at, 8), rows), :].astype(out.dtype)


def row_blocks(plan, inputs):
    q, width = inputs[0].shape
    cols = width * (len(inputs) // 4)
    full = pl.BlockSpec(memory_space=pltpu.VMEM)
    return pl.pallas_call(
        lambda *refs: rows_kernel(len(inputs) // 4, *refs),
        in_specs=[pl.BlockSpec(memory_space=pltpu.SMEM)] + [full] * len(inputs),
        out_specs=[full] * Z,
        out_shape=[jax.ShapeDtypeStruct((q // Z, cols), jnp.float32)]
        + [jax.ShapeDtypeStruct((q // Z, cols), jnp.bfloat16)] * (Z - 1),
        scratch_shapes=[pltpu.VMEM((q, cols), jnp.float32)],
        compiler_params=pltpu.CompilerParams(vmem_limit_bytes=32 * 2**20),
    )(plan, *inputs)


def sum_kernel(*refs):
    ins, (exact, rounded) = refs[:-2], refs[-2:]
    head = exact.shape[2]
    total = ins[0][...]
    for ref in ins[1:]:
        total = total + ref[...].astype(jnp.float32)
    for j in range(exact.shape[0]):
        block = total[:, j * head : (j + 1) * head]
        exact[j] = block
        rounded[j] = block.astype(rounded.dtype)


def sum_over_z(parts):
    rows, cols = parts[0].shape
    shape = (Z, rows, cols // Z)
    return pl.pallas_call(
        sum_kernel,
        out_shape=[
            jax.ShapeDtypeStruct(shape, jnp.float32),
            jax.ShapeDtypeStruct(shape, jnp.bfloat16),
        ],
    )(*parts)


def choose_kernel(place, *refs):
    ins, out = refs[:-1], refs[-1]
    for t in range(out.shape[0]):
        for d, ref in enumerate(ins):

            @pl.when(place[t] // Z == d)
            def _(t=t, ref=ref):
                out[t] = ref[lax.rem(place[t], Z)]


def choose(place, rows):
    full = pl.BlockSpec(memory_space=pltpu.VMEM)
    return pl.pallas_call(
        choose_kernel,
        in_specs=[pl.BlockSpec(memory_space=pltpu.SMEM)] + [full] * len(rows),
        out_specs=full,
        out_shape=jax.ShapeDtypeStruct(rows[0].shape, rows[0].dtype),
    )(place, *rows)


def polar_kernel(scale, g_ref, *refs):
    out_ref = refs[-1]
    gram = refs[0][...]
    for ref in refs[1:-1]:
        gram = gram + ref[...]

    def mul(a, b):
        return jnp.dot(a, b, precision=highest_precision_mode, preferred_element_type=jnp.float32)

    n = gram.shape[0]
    eye = (
        lax.broadcasted_iota(jnp.int32, (n, n), 0) == lax.broadcasted_iota(jnp.int32, (n, n), 1)
    ).astype(jnp.float32)
    norm = jnp.sqrt(jnp.sum(gram * eye, keepdims=True)) + norm_eps
    a1 = gram / norm / norm
    p1 = coeff_a * eye + coeff_b * a1 + coeff_c * mul(a1, a1)
    a2 = mul(mul(p1, a1), p1)
    p2 = coeff_a * eye + coeff_b * a2 + coeff_c * mul(a2, a2)
    mix = mul(p2, p1) * (scale / norm)
    out_ref[...] = mul(g_ref[...], mix).astype(out_ref.dtype)


def polar(g, grams):
    q, n = g.shape
    return pl.pallas_call(
        lambda *refs: polar_kernel(0.2 * math.sqrt(2 * DHALF), *refs),
        out_shape=jax.ShapeDtypeStruct((q, n), jnp.bfloat16),
        compiler_params=pltpu.CompilerParams(vmem_limit_bytes=16 * 2**20),
    )(g, *grams)


def on_device(
    mixer_vectors,
    upstream_adjoint,
    relative_benefit,
    present_policy_logit,
    behaviour_policy_logit,
    retained_entries,
    tallies,
    keeper_slot,
):
    bf16, f32 = jnp.bfloat16, jnp.float32
    yl, x, z = lax.axis_index("yl"), lax.axis_index("x"), lax.axis_index("z")
    yh, core = lax.axis_index("yh"), lax.axis_index("c")
    q = upstream_adjoint.shape[2]
    barrier = lax.optimization_barrier

    own = [pick_rows(retained_entries, mixer_vectors, piece, PIECES) for piece in range(PIECES)]
    adjoint = upstream_adjoint.transpose(1, 2, 0)
    kept, adjoint, *own = barrier((retained_entries, adjoint, *own))
    rows_of = [
        v[None, :] for v in (relative_benefit, present_policy_logit, behaviour_policy_logit)
    ]
    s_send = scaled_half(1 - yl, tallies[0], kept, *rows_of, adjoint)
    s_keep = scaled_half(yl, tallies[0], kept, *rows_of, adjoint)

    odd = (x + core) % 2
    near = jnp.where((x + odd) % X // 2 == yh, 0, 2)
    far = 2 - near
    plan = jnp.where(
        odd == 1,
        jnp.stack([near + 1, far, near, far + 1]),
        jnp.stack([far, far + 1, near + 1, near]),
    ).astype(jnp.int32)

    def add(*terms):
        return sum([t.astype(f32) for t in terms]).astype(bf16)

    def to_x(terms, ra, rb, beside=()):
        t2, t3 = terms[2:]
        rp = odd_to_even(add(t2, ra), 1)
        rm = odd_to_even(add(t3, rb), -1)
        t2, ra, rm, rp, *beside = barrier((t2, ra, rm, rp, *beside))
        return [even_to_odd_core(add(t2, ra, rm)), t3, rb, rp], beside

    e1, e3 = over_y(own[0], 1), over_y(own[0], 3)
    e1, e3, s_send, s_keep, second = barrier((e1, e3, s_send, s_keep, own[1]))
    opposite = over_y(e1, 3)
    s_recv = over_y(s_send, 1)
    c_keep = shift(s_keep, "c", C, 1)
    opposite, s_recv, c_keep, second = barrier((opposite, s_recv, c_keep, second))
    f1, f3 = over_y(second, 1), over_y(second, 3)
    c_recv = shift(s_recv, "c", C, 1)
    s_list = (s_keep, s_recv, c_keep, c_recv)
    first_terms = partials(plan, s_list, own[0], e1, e3, [opposite])
    cut = second.shape[0] // 2
    ra, rb = shift(first_terms[0], "x", X, 1), shift(first_terms[1], "x", X, -1)
    f1, f3, ra, rb = barrier((f1, f3, ra, rb))
    fa, fb = over_y(f3[:cut], 1), over_y(f1[cut:], 3)
    first_sums, (fa, fb) = to_x(first_terms, ra, rb, (fa, fb))
    second_terms = partials(plan, s_list, second, f1, f3, [fa, fb])
    ra, rb = shift(second_terms[0], "x", X, 1), shift(second_terms[1], "x", X, -1)
    second_sums, _ = to_x(second_terms, ra, rb)

    head = mixer_vectors.shape[1] // Z
    parts = row_blocks(jnp.stack([odd, z]).astype(jnp.int32), first_sums + second_sums)
    got = [shift(parts[d], "z", Z, d) for d in (4, 3, 5, 2, 6, 1, 7)]
    exact, rounded = sum_over_z([parts[0], *got])

    row_of = [rounded] + [shift(rounded, "x", X, d) for d in (1, 2, 3)]
    g = lax.all_to_all(exact, "z", 0, 0, tiled=True).reshape(q, head)
    gram = lax.dot_general(
        g, g, (((0,), (0,)), ((), ())), precision=highest_precision_mode,
        preferred_element_type=f32,
    )
    gram, rounded_rows = barrier((gram, row_of))
    gram = gram + shift(gram, "c", C, 1)
    update = polar(g, [gram] + [over_y(gram, flip) for flip in (2, 1, 3)])

    heads_total = keeper_slot.shape[0]
    heads = jnp.arange(heads_total, dtype=jnp.int32)
    wanted = x * Z + jnp.arange(Z, dtype=jnp.int32)
    source = jnp.sum(
        jnp.where(keeper_slot[None, :] == wanted[:, None], heads[None, :], 0), axis=1
    )
    place = ((x - source // Z) % X * Z + source % Z).astype(jnp.int32)
    chosen = choose(place, rounded_rows)
    arrived = lax.all_to_all(chosen, "z", 0, 0, tiled=True).reshape(q, head)
    gradient = arrived.astype(f32).T
    return (update.T[None], gradient[None])


def solution(mesh):
    wide = Mesh(np.asarray(mesh.devices).reshape(YL, X, Z, YH, C), NAMES)
    dp, mp = ("yl", "x", "z"), ("yh", "c")
    return jax.shard_map(
        on_device,
        mesh=wide,
        in_specs=(
            P(dp, mp),
            P(dp, None, mp),
            P(dp),
            P(dp),
            P(dp),
            P(dp, None),
            P(dp),
            P(),
        ),
        out_specs=(P(dp, None, mp), P(dp, None, mp)),
        check_vma=False,
    )
```

```python
import math

import jax
import jax.numpy as jnp
import numpy as np
from jax import lax
from jax.experimental import pallas as pl
from jax.experimental.pallas import tpu as pltpu
from jax.sharding import Mesh
from jax.sharding import PartitionSpec as P

DHALF = 1792

coeff_a = 3.4445
coeff_b = -4.775
coeff_c = 2.0315
norm_eps = 1e-06
highest_precision_mode = lax.Precision.HIGHEST

YL, X, Z, YH, C = 2, 4, 8, 2, 2
NAMES = ("yl", "x", "z", "yh", "c")
FIRST = 640


def ring_pairs(flip):
    def index(y):
        return (y % 2) * 2 + y // 2

    return [(index(y), index(y ^ flip)) for y in range(4)]


def over_y(value, flip):
    return lax.ppermute(value, ("yl", "yh"), ring_pairs(flip))


def shift(value, axis, size, step):
    return lax.ppermute(value, axis, [(i, (i + step) % size) for i in range(size)])


def over_xc(value, odd_step, odd_flip, even_step=None, even_flip=0):
    pairs = []
    for x in range(X):
        for c in range(C):
            step, flip = (odd_step, odd_flip) if (x + c) % 2 else (even_step, even_flip)
            if step is not None:
                pairs.append((x * C + c, (x + step) % X * C + (c ^ flip)))
    return lax.ppermute(value, ("x", "c"), pairs)


def pick_kernel(columns, kept_ref, v_ref, out_ref):
    rows, cap = v_ref.shape[0], kept_ref.shape[1]
    column = jnp.broadcast_to(kept_ref[...], (8, cap)).T[:, :1]
    pick = lax.broadcasted_iota(jnp.int32, (cap, rows), 1) == column
    out_ref[...] = jnp.dot(
        pick.astype(jnp.bfloat16), v_ref[:, columns], preferred_element_type=jnp.float32
    ).astype(out_ref.dtype)


def pick_rows(kept, values, start, stop):
    rows = values.shape[0]
    cap = kept.shape[1]
    width = stop - start
    full = pl.BlockSpec(memory_space=pltpu.VMEM)
    return pl.pallas_call(
        lambda *refs: pick_kernel(slice(start, stop), *refs),
        in_specs=[full] * 2,
        out_specs=full,
        out_shape=jax.ShapeDtypeStruct((cap, width), values.dtype),
        compiler_params=pltpu.CompilerParams(vmem_limit_bytes=16 * 2**20),
        cost_estimate=pl.CostEstimate(
            flops=2 * cap * rows * width, bytes_accessed=2 * (rows + cap) * width, transcendentals=0
        ),
    )(kept, values)


def scale_kernel(plan, kept_ref, benefit_ref, present_ref, behaviour_ref, u_ref, out_ref):
    rows, cap = u_ref.shape[2], kept_ref.shape[1]
    pick = (lax.broadcasted_iota(jnp.int32, (rows, cap), 0) == kept_ref[...]).astype(jnp.bfloat16)
    rest = benefit_ref[...] * jnp.exp(present_ref[...] - behaviour_ref[...])
    parts = []
    for _ in range(3):
        part = rest.astype(jnp.bfloat16)
        parts.append(part)
        rest = rest - part.astype(jnp.float32)
    weight = jnp.zeros((1, cap), jnp.float32)
    for part in parts[::-1]:
        stacked = jnp.broadcast_to(part, (16, rows))
        weight = weight + jnp.dot(stacked, pick, preferred_element_type=jnp.float32)[:1]
    live = lax.broadcasted_iota(jnp.int32, (1, cap), 1) < plan[1]
    weight = jnp.where(live, weight, 0.0)
    picked = jnp.dot(u_ref[0], pick, preferred_element_type=jnp.float32)
    out_ref[...] = (weight * picked).astype(out_ref.dtype)


def scaled_half(half, tally, kept, benefit, present, behaviour, adjoint):
    _, q, rows = adjoint.shape
    cap = kept.shape[1]
    row_spec = pl.BlockSpec((1, rows), lambda i, plan: (0, 0))
    return pl.pallas_call(
        scale_kernel,
        grid_spec=pltpu.PrefetchScalarGridSpec(
            num_scalar_prefetch=1,
            grid=(1,),
            in_specs=[
                pl.BlockSpec((1, cap), lambda i, plan: (0, 0)),
                row_spec,
                row_spec,
                row_spec,
                pl.BlockSpec((1, q, rows), lambda i, plan: (plan[0], 0, 0)),
            ],
            out_specs=pl.BlockSpec((q, cap), lambda i, plan: (0, 0)),
        ),
        out_shape=jax.ShapeDtypeStruct((q, cap), jnp.bfloat16),
        compiler_params=pltpu.CompilerParams(vmem_limit_bytes=20 * 2**20),
        cost_estimate=pl.CostEstimate(
            flops=2 * q * rows * cap, bytes_accessed=2 * q * (rows + cap), transcendentals=rows
        ),
    )(jnp.stack([half, tally]).astype(jnp.int32), kept, benefit, present, behaviour, adjoint)


def partial_kernel(counts, plan, *refs):
    s_refs, out_refs = refs[:4], refs[-6:-2]
    s_all, total = refs[-2:]
    q, cap = s_refs[0].shape
    for i, ref in enumerate(s_refs):
        side, other = divmod(i, 2)
        s_all[side * q : (side + 1) * q, other * cap : (other + 1) * cap] = ref[...]

    at = 4
    for chunk in range(2):
        value = None
        for other in range(2):
            count = counts[2 * chunk + other]
            blocks = [ref[...] for ref in refs[at : at + count]]
            at += count
            block = blocks[0] if count == 1 else jnp.concatenate(blocks, axis=0)
            term = jnp.dot(
                s_all[:, other * cap : (other + 1) * cap],
                block,
                preferred_element_type=jnp.float32,
            )
            value = term if value is None else value + term
        value = value.astype(total.dtype)
        for side in range(2):
            total[2 * chunk + side] = value[side * q : (side + 1) * q]
    for slot, out_ref in enumerate(out_refs):
        out_ref[...] = total[plan[slot]]


def partials(plan, s_list, own, e1, opposite, e3, after=()):
    q, cap = s_list[0].shape
    cols = own[0].shape[1]
    groups = (own, e1, opposite, e3)
    counts = tuple(len(group) for group in groups)
    values = [block for group in groups for block in group]
    full = pl.BlockSpec(memory_space=pltpu.VMEM)
    return pl.pallas_call(
        lambda *refs: partial_kernel(counts, *refs),
        in_specs=[pl.BlockSpec(memory_space=pltpu.SMEM)]
        + [full] * (4 + len(values))
        + [pl.BlockSpec(memory_space=pl.ANY)] * len(after),
        out_specs=[full] * 4,
        scratch_shapes=[
            pltpu.VMEM((2 * q, 2 * cap), jnp.bfloat16),
            pltpu.VMEM((4, q, cols), jnp.bfloat16),
        ],
        out_shape=[jax.ShapeDtypeStruct((q, cols), jnp.bfloat16)] * 4,
        compiler_params=pltpu.CompilerParams(vmem_limit_bytes=20 * 2**20),
        cost_estimate=pl.CostEstimate(
            flops=8 * q * 2 * cap * cols, bytes_accessed=8 * 2**20, transcendentals=0
        ),
    )(plan, *s_list, *values, *after)


def rows_kernel(piece_count, plan, *refs):
    ins, outs, mine = refs[: 5 * piece_count], refs[5 * piece_count : -1], refs[-1]
    start = 0
    for piece in range(piece_count):
        *got, last, kept = ins[5 * piece : 5 * piece + 5]
        columns = slice(start, start + kept.shape[1])
        start += kept.shape[1]
        total = got[0][...].astype(jnp.float32)
        for ref in got[1:]:
            total = total + ref[...].astype(jnp.float32)

        @pl.when(plan[0] == 1)
        def _(total=total, last=last, columns=columns):
            mine[:, columns] = total + last[...].astype(jnp.float32)

        @pl.when(plan[0] == 0)
        def _(total=total, kept=kept, columns=columns):
            mine[:, columns] = total + kept[...].astype(jnp.float32)

    for step, out in enumerate(outs):
        heads, rows, head = out.shape
        at = pl.multiple_of(lax.rem(plan[1] + step, Z) * rows, 8)
        for j in range(heads):
            out[j] = mine[pl.ds(at, rows), j * head : (j + 1) * head].astype(out.dtype)


def row_blocks(plan, inputs):
    q = inputs[0].shape[0]
    cols = sum(t.shape[1] for t in inputs[::5])
    shape = (Z, q // Z, cols // Z)
    full = pl.BlockSpec(memory_space=pltpu.VMEM)
    return pl.pallas_call(
        lambda *refs: rows_kernel(len(inputs) // 5, *refs),
        in_specs=[pl.BlockSpec(memory_space=pltpu.SMEM)] + [full] * len(inputs),
        out_specs=[full] * Z,
        out_shape=[jax.ShapeDtypeStruct(shape, jnp.float32)]
        + [jax.ShapeDtypeStruct(shape, jnp.bfloat16)] * (Z - 1),
        scratch_shapes=[pltpu.VMEM((q, cols), jnp.float32)],
        compiler_params=pltpu.CompilerParams(vmem_limit_bytes=16 * 2**20),
    )(plan, *inputs)


def choose_kernel(place, *refs):
    ins, out = refs[:-1], refs[-1]
    for t in range(out.shape[0]):
        for d, ref in enumerate(ins):

            @pl.when(place[t] // Z == d)
            def _(t=t, ref=ref):
                out[t] = ref[lax.rem(place[t], Z)]


def choose(place, rows):
    full = pl.BlockSpec(memory_space=pltpu.VMEM)
    return pl.pallas_call(
        choose_kernel,
        in_specs=[pl.BlockSpec(memory_space=pltpu.SMEM)] + [full] * len(rows),
        out_specs=full,
        out_shape=jax.ShapeDtypeStruct(rows[0].shape, rows[0].dtype),
    )(place, *rows)


def polar_kernel(scale, g_ref, *refs):
    out_ref = refs[-1]
    gram = refs[0][...]
    for ref in refs[1:-1]:
        gram = gram + ref[...]

    def mul(a, b):
        return jnp.dot(a, b, precision=highest_precision_mode, preferred_element_type=jnp.float32)

    n = gram.shape[0]
    eye = (
        lax.broadcasted_iota(jnp.int32, (n, n), 0) == lax.broadcasted_iota(jnp.int32, (n, n), 1)
    ).astype(jnp.float32)
    norm = jnp.sqrt(jnp.sum(gram * eye, keepdims=True)) + norm_eps
    a1 = gram / norm / norm
    p1 = coeff_a * eye + coeff_b * a1 + coeff_c * mul(a1, a1)
    a2 = mul(mul(p1, a1), p1)
    p2 = coeff_a * eye + coeff_b * a2 + coeff_c * mul(a2, a2)
    mix = mul(p2, p1) * (scale / norm)
    out_ref[...] = mul(g_ref[...], mix).astype(out_ref.dtype)


def polar(g, grams):
    q, n = g.shape
    return pl.pallas_call(
        lambda *refs: polar_kernel(0.2 * math.sqrt(2 * DHALF), *refs),
        out_shape=jax.ShapeDtypeStruct((q, n), jnp.bfloat16),
        compiler_params=pltpu.CompilerParams(vmem_limit_bytes=16 * 2**20),
    )(g, *grams)


def on_device(
    mixer_vectors,
    upstream_adjoint,
    relative_benefit,
    present_policy_logit,
    behaviour_policy_logit,
    retained_entries,
    tallies,
    keeper_slot,
):
    bf16, f32 = jnp.bfloat16, jnp.float32
    yl, x, z = lax.axis_index("yl"), lax.axis_index("x"), lax.axis_index("z")
    yh, core = lax.axis_index("yh"), lax.axis_index("c")
    q = upstream_adjoint.shape[2]
    barrier = lax.optimization_barrier

    own = [
        pick_rows(retained_entries, mixer_vectors, start, stop)
        for start, stop in ((0, FIRST), (FIRST, mixer_vectors.shape[1]))
    ]
    adjoint = upstream_adjoint.transpose(1, 2, 0)
    kept, adjoint, *own = barrier((retained_entries, adjoint, *own))
    rows_of = [
        v[None, :] for v in (relative_benefit, present_policy_logit, behaviour_policy_logit)
    ]
    s_send = scaled_half(1 - yl, tallies[0], kept, *rows_of, adjoint)
    s_keep = scaled_half(yl, tallies[0], kept, *rows_of, adjoint)

    odd = (x + core) % 2
    near = jnp.where((x + odd) % X // 2 == yh, 0, 2)
    far = 2 - near
    plan = jnp.where(
        odd == 1,
        jnp.stack([near, far, near + 1, far + 1]),
        jnp.stack([far + 1, near + 1, far, near]),
    ).astype(jnp.int32)

    def over_x(terms):
        return [
            over_xc(terms[0], 1, 0, 2, 1),
            over_xc(terms[1], -1, 0, 0, 1),
            over_xc(terms[2], 1, 1, 2, 0),
            over_xc(terms[3], -1, 1),
            terms[3],
        ]

    e1, e3 = over_y(own[0], 1), over_y(own[0], 3)
    e1, e3, s_send, s_keep, second = barrier((e1, e3, s_send, s_keep, own[1]))
    opposite = over_y(e1, 3)
    s_recv = over_y(s_send, 1)
    c_keep = shift(s_keep, "c", C, 1)
    opposite, s_recv, c_keep, second = barrier((opposite, s_recv, c_keep, second))
    f1, f3 = over_y(second, 1), over_y(second, 3)
    c_recv = shift(s_recv, "c", C, 1)
    s_list = (s_keep, s_recv, c_keep, c_recv)
    first_terms = partials(plan, s_list, [own[0]], [e1], [opposite], [e3])
    first_sums = over_x(first_terms)
    cut = second.shape[0] // 2
    fa, fb = over_y(f3[:cut], 1), over_y(f1[cut:], 3)
    second_terms = partials(plan, s_list, [second], [f1], [fa, fb], [f3], first_sums[:1])
    second_sums = over_x(second_terms)

    head = mixer_vectors.shape[1] // Z
    parts = row_blocks(jnp.stack([odd, z]).astype(jnp.int32), first_sums + second_sums)
    exact = parts[0]
    for got in [shift(parts[d], "z", Z, d) for d in (4, 3, 5, 2, 6, 1, 7)]:
        exact = exact + got.astype(f32)
    rounded = exact.astype(bf16)

    heads_total = keeper_slot.shape[0]
    heads = jnp.arange(heads_total, dtype=jnp.int32)
    wanted = x * Z + jnp.arange(Z, dtype=jnp.int32)
    source = jnp.sum(
        jnp.where(keeper_slot[None, :] == wanted[:, None], heads[None, :], 0), axis=1
    )
    place = ((x - source // Z) % X * Z + source % Z).astype(jnp.int32)
    chosen = choose(place, [rounded] + [shift(rounded, "x", X, d) for d in (1, 2, 3)])
    arrived = lax.all_to_all(chosen, "z", 0, 0, tiled=True).reshape(q, head)

    g = lax.all_to_all(exact, "z", 0, 0, tiled=True).reshape(q, head)
    gram = lax.dot_general(
        g, g, (((0,), (0,)), ((), ())), precision=highest_precision_mode,
        preferred_element_type=f32,
    )
    gram = gram + shift(gram, "c", C, 1)
    update = polar(g, [gram] + [over_y(gram, flip) for flip in (2, 1, 3)])
    gradient = arrived.astype(f32).T
    return (update.T[None], gradient[None])


def solution(mesh):
    wide = Mesh(np.asarray(mesh.devices).reshape(YL, X, Z, YH, C), NAMES)
    dp, mp = ("yl", "x", "z"), ("yh", "c")
    return jax.shard_map(
        on_device,
        mesh=wide,
        in_specs=(
            P(dp, mp),
            P(dp, None, mp),
            P(dp),
            P(dp),
            P(dp),
            P(dp, None),
            P(dp),
            P(),
        ),
        out_specs=(P(dp, None, mp), P(dp, None, mp)),
        check_vma=False,
    )
```

```python
import math

import jax
import jax.numpy as jnp
import numpy as np
from jax import lax
from jax.experimental import pallas as pl
from jax.experimental.pallas import tpu as pltpu
from jax.sharding import Mesh
from jax.sharding import PartitionSpec as P

DHALF = 1792

coeff_a = 3.4445
coeff_b = -4.775
coeff_c = 2.0315
norm_eps = 1e-06
highest_precision_mode = lax.Precision.HIGHEST

YL, X, Z, YH, C = 2, 4, 8, 2, 2
NAMES = ("yl", "x", "z", "yh", "c")
FIRST = 640


def ring_pairs(flip):
    def index(y):
        return (y % 2) * 2 + y // 2

    return [(index(y), index(y ^ flip)) for y in range(4)]


def over_y(value, flip):
    return lax.ppermute(value, ("yl", "yh"), ring_pairs(flip))


def shift(value, axis, size, step):
    return lax.ppermute(value, axis, [(i, (i + step) % size) for i in range(size)])


def over_xc(value, odd_step, odd_flip, even_step=None, even_flip=0):
    pairs = []
    for x in range(X):
        for c in range(C):
            step, flip = (odd_step, odd_flip) if (x + c) % 2 else (even_step, even_flip)
            if step is not None:
                pairs.append((x * C + c, (x + step) % X * C + (c ^ flip)))
    return lax.ppermute(value, ("x", "c"), pairs)


def pick_kernel(columns, kept_ref, v_ref, out_ref):
    rows, cap = v_ref.shape[0], kept_ref.shape[1]
    column = jnp.broadcast_to(kept_ref[...], (8, cap)).T[:, :1]
    pick = lax.broadcasted_iota(jnp.int32, (cap, rows), 1) == column
    out_ref[...] = jnp.dot(
        pick.astype(jnp.bfloat16), v_ref[:, columns], preferred_element_type=jnp.float32
    ).astype(out_ref.dtype)


def pick_rows(kept, values, start, stop):
    rows = values.shape[0]
    cap = kept.shape[1]
    width = stop - start
    full = pl.BlockSpec(memory_space=pltpu.VMEM)
    return pl.pallas_call(
        lambda *refs: pick_kernel(slice(start, stop), *refs),
        in_specs=[full] * 2,
        out_specs=full,
        out_shape=jax.ShapeDtypeStruct((cap, width), values.dtype),
        compiler_params=pltpu.CompilerParams(vmem_limit_bytes=16 * 2**20),
        cost_estimate=pl.CostEstimate(
            flops=2 * cap * rows * width, bytes_accessed=2 * (rows + cap) * width, transcendentals=0
        ),
    )(kept, values)


def scale_kernel(plan, kept_ref, benefit_ref, present_ref, behaviour_ref, u_ref, out_ref):
    rows, cap = u_ref.shape[2], kept_ref.shape[1]
    pick = (lax.broadcasted_iota(jnp.int32, (rows, cap), 0) == kept_ref[...]).astype(jnp.bfloat16)
    rest = benefit_ref[...] * jnp.exp(present_ref[...] - behaviour_ref[...])
    parts = []
    for _ in range(3):
        part = rest.astype(jnp.bfloat16)
        parts.append(part)
        rest = rest - part.astype(jnp.float32)
    weight = jnp.zeros((1, cap), jnp.float32)
    for part in parts[::-1]:
        stacked = jnp.broadcast_to(part, (16, rows))
        weight = weight + jnp.dot(stacked, pick, preferred_element_type=jnp.float32)[:1]
    live = lax.broadcasted_iota(jnp.int32, (1, cap), 1) < plan[1]
    weight = jnp.where(live, weight, 0.0)
    picked = jnp.dot(u_ref[0], pick, preferred_element_type=jnp.float32)
    out_ref[...] = (weight * picked).astype(out_ref.dtype)


def scaled_half(half, tally, kept, benefit, present, behaviour, adjoint):
    _, q, rows = adjoint.shape
    cap = kept.shape[1]
    row_spec = pl.BlockSpec((1, rows), lambda i, plan: (0, 0))
    return pl.pallas_call(
        scale_kernel,
        grid_spec=pltpu.PrefetchScalarGridSpec(
            num_scalar_prefetch=1,
            grid=(1,),
            in_specs=[
                pl.BlockSpec((1, cap), lambda i, plan: (0, 0)),
                row_spec,
                row_spec,
                row_spec,
                pl.BlockSpec((1, q, rows), lambda i, plan: (plan[0], 0, 0)),
            ],
            out_specs=pl.BlockSpec((q, cap), lambda i, plan: (0, 0)),
        ),
        out_shape=jax.ShapeDtypeStruct((q, cap), jnp.bfloat16),
        compiler_params=pltpu.CompilerParams(vmem_limit_bytes=20 * 2**20),
        cost_estimate=pl.CostEstimate(
            flops=2 * q * rows * cap, bytes_accessed=2 * q * (rows + cap), transcendentals=rows
        ),
    )(jnp.stack([half, tally]).astype(jnp.int32), kept, benefit, present, behaviour, adjoint)


def partial_kernel(counts, plan, *refs):
    total, refs = refs[-1], refs[:-1]
    if len(counts) == 5:
        s_refs, out_refs, s_all = refs[:4], refs[-5:-1], refs[-1]
        q, cap = s_refs[0].shape
        for i, ref in enumerate(s_refs):
            side, other = divmod(i, 2)
            s_all[side * q : (side + 1) * q, other * cap : (other + 1) * cap] = ref[...]
        at = 4
    else:
        out_refs, s_all = refs[-4:], refs[0]
        q, cap = s_all.shape[0] // 2, s_all.shape[1] // 2
        at = 1

    for chunk in range(2):
        value = None
        for other in range(2):
            count = counts[2 * chunk + other]
            blocks = [ref[...] for ref in refs[at : at + count]]
            at += count
            block = blocks[0] if count == 1 else jnp.concatenate(blocks, axis=0)
            term = jnp.dot(
                s_all[:, other * cap : (other + 1) * cap],
                block,
                preferred_element_type=jnp.float32,
            )
            value = term if value is None else value + term
        value = value.astype(total.dtype)
        for side in range(2):
            total[2 * chunk + side] = value[side * q : (side + 1) * q]
    for slot, out_ref in enumerate(out_refs):
        out_ref[...] = total[plan[slot]]


def partials(plan, s_list, own, e1, opposite, e3, after=()):
    if len(s_list) == 4:
        q, cap = s_list[0].shape
    else:
        q, cap = s_list[0].shape[0] // 2, s_list[0].shape[1] // 2
    cols = own[0].shape[1]
    groups = (own, e1, opposite, e3)
    counts = tuple(len(group) for group in groups)
    values = [block for group in groups for block in group]
    full = pl.BlockSpec(memory_space=pltpu.VMEM)
    shapes = [jax.ShapeDtypeStruct((q, cols), jnp.bfloat16)] * 4
    if len(s_list) == 4:
        shapes.append(jax.ShapeDtypeStruct((2 * q, 2 * cap), jnp.bfloat16))
        counts += (1,)
    return pl.pallas_call(
        lambda *refs: partial_kernel(counts, *refs),
        in_specs=[pl.BlockSpec(memory_space=pltpu.SMEM)]
        + [full] * (len(s_list) + len(values))
        + [pl.BlockSpec(memory_space=pl.ANY)] * len(after),
        out_specs=[full] * len(shapes),
        scratch_shapes=[pltpu.VMEM((4, q, cols), jnp.bfloat16)],
        out_shape=shapes,
        compiler_params=pltpu.CompilerParams(vmem_limit_bytes=20 * 2**20),
        cost_estimate=pl.CostEstimate(
            flops=8 * q * 2 * cap * cols, bytes_accessed=8 * 2**20, transcendentals=0
        ),
    )(plan, *s_list, *values, *after)


def rows_kernel(piece_count, plan, *refs):
    ins, outs, mine = refs[: 5 * piece_count], refs[5 * piece_count : -1], refs[-1]
    start = 0
    for piece in range(piece_count):
        *got, last, kept = ins[5 * piece : 5 * piece + 5]
        columns = slice(start, start + kept.shape[1])
        start += kept.shape[1]
        total = got[0][...].astype(jnp.float32)
        for ref in got[1:]:
            total = total + ref[...].astype(jnp.float32)

        @pl.when(plan[0] == 1)
        def _(total=total, last=last, columns=columns):
            mine[:, columns] = total + last[...].astype(jnp.float32)

        @pl.when(plan[0] == 0)
        def _(total=total, kept=kept, columns=columns):
            mine[:, columns] = total + kept[...].astype(jnp.float32)

    for step, out in enumerate(outs):
        heads, rows, head = out.shape
        at = pl.multiple_of(lax.rem(plan[1] + step, Z) * rows, 8)
        for j in range(heads):
            out[j] = mine[pl.ds(at, rows), j * head : (j + 1) * head].astype(out.dtype)


def row_blocks(plan, inputs):
    q = inputs[0].shape[0]
    cols = sum(t.shape[1] for t in inputs[::5])
    shape = (Z, q // Z, cols // Z)
    full = pl.BlockSpec(memory_space=pltpu.VMEM)
    return pl.pallas_call(
        lambda *refs: rows_kernel(len(inputs) // 5, *refs),
        in_specs=[pl.BlockSpec(memory_space=pltpu.SMEM)] + [full] * len(inputs),
        out_specs=[full] * Z,
        out_shape=[jax.ShapeDtypeStruct(shape, jnp.float32)]
        + [jax.ShapeDtypeStruct(shape, jnp.bfloat16)] * (Z - 1),
        scratch_shapes=[pltpu.VMEM((q, cols), jnp.float32)],
        compiler_params=pltpu.CompilerParams(vmem_limit_bytes=16 * 2**20),
    )(plan, *inputs)


def choose_kernel(place, *refs):
    ins, out = refs[:-1], refs[-1]
    for t in range(out.shape[0]):
        for d, ref in enumerate(ins):

            @pl.when(place[t] // Z == d)
            def _(t=t, ref=ref):
                out[t] = ref[lax.rem(place[t], Z)]


def choose(place, rows):
    full = pl.BlockSpec(memory_space=pltpu.VMEM)
    return pl.pallas_call(
        choose_kernel,
        in_specs=[pl.BlockSpec(memory_space=pltpu.SMEM)] + [full] * len(rows),
        out_specs=full,
        out_shape=jax.ShapeDtypeStruct(rows[0].shape, rows[0].dtype),
    )(place, *rows)


def polar_kernel(scale, g_ref, *refs):
    out_ref = refs[-1]
    gram = refs[0][...]
    for ref in refs[1:-1]:
        gram = gram + ref[...]

    def mul(a, b):
        return jnp.dot(a, b, precision=highest_precision_mode, preferred_element_type=jnp.float32)

    n = gram.shape[0]
    eye = (
        lax.broadcasted_iota(jnp.int32, (n, n), 0) == lax.broadcasted_iota(jnp.int32, (n, n), 1)
    ).astype(jnp.float32)
    norm = jnp.sqrt(jnp.sum(gram * eye, keepdims=True)) + norm_eps
    a1 = gram / norm / norm
    p1 = coeff_a * eye + coeff_b * a1 + coeff_c * mul(a1, a1)
    a2 = mul(mul(p1, a1), p1)
    p2 = coeff_a * eye + coeff_b * a2 + coeff_c * mul(a2, a2)
    mix = mul(p2, p1) * (scale / norm)
    out_ref[...] = mul(g_ref[...], mix).astype(out_ref.dtype)


def polar(g, grams):
    q, n = g.shape
    return pl.pallas_call(
        lambda *refs: polar_kernel(0.2 * math.sqrt(2 * DHALF), *refs),
        out_shape=jax.ShapeDtypeStruct((q, n), jnp.bfloat16),
        compiler_params=pltpu.CompilerParams(vmem_limit_bytes=16 * 2**20),
    )(g, *grams)


def on_device(
    mixer_vectors,
    upstream_adjoint,
    relative_benefit,
    present_policy_logit,
    behaviour_policy_logit,
    retained_entries,
    tallies,
    keeper_slot,
):
    bf16, f32 = jnp.bfloat16, jnp.float32
    yl, x, z = lax.axis_index("yl"), lax.axis_index("x"), lax.axis_index("z")
    yh, core = lax.axis_index("yh"), lax.axis_index("c")
    q = upstream_adjoint.shape[2]
    barrier = lax.optimization_barrier

    own = [
        pick_rows(retained_entries, mixer_vectors, start, stop)
        for start, stop in ((0, FIRST), (FIRST, mixer_vectors.shape[1]))
    ]
    adjoint = upstream_adjoint.transpose(1, 2, 0)
    kept, adjoint, own[0] = barrier((retained_entries, adjoint, own[0]))
    rows_of = [
        v[None, :] for v in (relative_benefit, present_policy_logit, behaviour_policy_logit)
    ]
    s_send = scaled_half(1 - yl, tallies[0], kept, *rows_of, adjoint)
    s_keep = scaled_half(yl, tallies[0], kept, *rows_of, adjoint)

    odd = (x + core) % 2
    near = jnp.where((x + odd) % X // 2 == yh, 0, 2)
    far = 2 - near
    plan = jnp.where(
        odd == 1,
        jnp.stack([near, far, near + 1, far + 1]),
        jnp.stack([far + 1, near + 1, far, near]),
    ).astype(jnp.int32)

    def over_x(terms):
        return [
            over_xc(terms[0], 1, 0, 2, 1),
            over_xc(terms[1], -1, 0, 0, 1),
            over_xc(terms[2], 1, 1, 2, 0),
            over_xc(terms[3], -1, 1),
            terms[3],
        ]

    e1, e3 = over_y(own[0], 1), over_y(own[0], 3)
    e1, e3, s_send, s_keep = barrier((e1, e3, s_send, s_keep))
    opposite = over_y(e1, 3)
    s_recv = over_y(s_send, 1)
    c_keep = shift(s_keep, "c", C, 1)
    opposite, s_recv, c_keep, second = barrier((opposite, s_recv, c_keep, own[1]))
    f1, f3 = over_y(second, 1), over_y(second, 3)
    c_recv = shift(s_recv, "c", C, 1)
    s_list = (s_keep, s_recv, c_keep, c_recv)
    *first_terms, s_all = partials(plan, s_list, [own[0]], [e1], [opposite], [e3])
    first_sums = over_x(first_terms)
    cut = second.shape[0] // 2
    fa, fb = over_y(f3[:cut], 1), over_y(f1[cut:], 3)
    second_terms = partials(plan, [s_all], [second], [f1], [fa, fb], [f3], first_sums[:1])
    second_sums = over_x(second_terms)

    head = mixer_vectors.shape[1] // Z
    parts = row_blocks(jnp.stack([odd, z]).astype(jnp.int32), first_sums + second_sums)
    exact = parts[0]
    for got in [shift(parts[d], "z", Z, d) for d in (4, 3, 5, 2, 6, 1, 7)]:
        exact = exact + got.astype(f32)
    rounded = exact.astype(bf16)

    heads_total = keeper_slot.shape[0]
    heads = jnp.arange(heads_total, dtype=jnp.int32)
    wanted = x * Z + jnp.arange(Z, dtype=jnp.int32)
    source = jnp.sum(
        jnp.where(keeper_slot[None, :] == wanted[:, None], heads[None, :], 0), axis=1
    )
    place = ((x - source // Z) % X * Z + source % Z).astype(jnp.int32)
    chosen = choose(place, [rounded] + [shift(rounded, "x", X, d) for d in (1, 2, 3)])
    arrived = lax.all_to_all(chosen, "z", 0, 0, tiled=True).reshape(q, head)

    g = lax.all_to_all(exact, "z", 0, 0, tiled=True).reshape(q, head)
    gram = lax.dot_general(
        g, g, (((0,), (0,)), ((), ())), precision=highest_precision_mode,
        preferred_element_type=f32,
    )
    gram = gram + shift(gram, "c", C, 1)
    update = polar(g, [gram] + [over_y(gram, flip) for flip in (2, 1, 3)])
    gradient = arrived.astype(f32).T
    return (update.T[None], gradient[None])


def solution(mesh):
    wide = Mesh(np.asarray(mesh.devices).reshape(YL, X, Z, YH, C), NAMES)
    dp, mp = ("yl", "x", "z"), ("yh", "c")
    return jax.shard_map(
        on_device,
        mesh=wide,
        in_specs=(
            P(dp, mp),
            P(dp, None, mp),
            P(dp),
            P(dp),
            P(dp),
            P(dp, None),
            P(dp),
            P(),
        ),
        out_specs=(P(dp, None, mp), P(dp, None, mp)),
        check_vma=False,
    )
```

```python
import math

import jax
import jax.numpy as jnp
import numpy as np
from jax import lax
from jax.experimental import pallas as pl
from jax.experimental.pallas import tpu as pltpu
from jax.sharding import Mesh
from jax.sharding import PartitionSpec as P

DHALF = 1792

coeff_a = 3.4445
coeff_b = -4.775
coeff_c = 2.0315
norm_eps = 1e-06
highest_precision_mode = lax.Precision.HIGHEST

YL, X, Z, YH, C = 2, 4, 8, 2, 2
NAMES = ("yl", "x", "z", "yh", "c")
FIRST = 640


def ring_pairs(flip):
    def index(y):
        return (y % 2) * 2 + y // 2

    return [(index(y), index(y ^ flip)) for y in range(4)]


def over_y(value, flip):
    return lax.ppermute(value, ("yl", "yh"), ring_pairs(flip))


def shift(value, axis, size, step):
    return lax.ppermute(value, axis, [(i, (i + step) % size) for i in range(size)])


def over_xc(value, odd_step, odd_flip, even_step=None, even_flip=0):
    pairs = []
    for x in range(X):
        for c in range(C):
            step, flip = (odd_step, odd_flip) if (x + c) % 2 else (even_step, even_flip)
            if step is not None:
                pairs.append((x * C + c, (x + step) % X * C + (c ^ flip)))
    return lax.ppermute(value, ("x", "c"), pairs)


def pick_kernel(columns, kept_ref, v_ref, out_ref):
    rows, cap = v_ref.shape[0], kept_ref.shape[1]
    column = jnp.broadcast_to(kept_ref[...], (8, cap)).T[:, :1]
    pick = lax.broadcasted_iota(jnp.int32, (cap, rows), 1) == column
    out_ref[...] = jnp.dot(
        pick.astype(jnp.bfloat16), v_ref[:, columns], preferred_element_type=jnp.float32
    ).astype(out_ref.dtype)


def pick_rows(kept, values, start, stop):
    rows = values.shape[0]
    cap = kept.shape[1]
    width = stop - start
    full = pl.BlockSpec(memory_space=pltpu.VMEM)
    return pl.pallas_call(
        lambda *refs: pick_kernel(slice(start, stop), *refs),
        in_specs=[full] * 2,
        out_specs=full,
        out_shape=jax.ShapeDtypeStruct((cap, width), values.dtype),
        compiler_params=pltpu.CompilerParams(vmem_limit_bytes=16 * 2**20),
        cost_estimate=pl.CostEstimate(
            flops=2 * cap * rows * width, bytes_accessed=2 * (rows + cap) * width, transcendentals=0
        ),
    )(kept, values)


def scale_kernel(plan, kept_ref, benefit_ref, present_ref, behaviour_ref, u_ref, out_ref):
    rows, cap = u_ref.shape[2], kept_ref.shape[1]
    pick = (lax.broadcasted_iota(jnp.int32, (rows, cap), 0) == kept_ref[...]).astype(jnp.bfloat16)
    rest = benefit_ref[...] * jnp.exp(present_ref[...] - behaviour_ref[...])
    parts = []
    for _ in range(3):
        part = rest.astype(jnp.bfloat16)
        parts.append(part)
        rest = rest - part.astype(jnp.float32)
    weight = jnp.zeros((1, cap), jnp.float32)
    for part in parts[::-1]:
        stacked = jnp.broadcast_to(part, (16, rows))
        weight = weight + jnp.dot(stacked, pick, preferred_element_type=jnp.float32)[:1]
    live = lax.broadcasted_iota(jnp.int32, (1, cap), 1) < plan[1]
    weight = jnp.where(live, weight, 0.0)
    picked = jnp.dot(u_ref[0], pick, preferred_element_type=jnp.float32)
    out_ref[...] = (weight * picked).astype(out_ref.dtype)


def scaled_half(half, tally, kept, benefit, present, behaviour, adjoint):
    _, q, rows = adjoint.shape
    cap = kept.shape[1]
    row_spec = pl.BlockSpec((1, rows), lambda i, plan: (0, 0))
    return pl.pallas_call(
        scale_kernel,
        grid_spec=pltpu.PrefetchScalarGridSpec(
            num_scalar_prefetch=1,
            grid=(1,),
            in_specs=[
                pl.BlockSpec((1, cap), lambda i, plan: (0, 0)),
                row_spec,
                row_spec,
                row_spec,
                pl.BlockSpec((1, q, rows), lambda i, plan: (plan[0], 0, 0)),
            ],
            out_specs=pl.BlockSpec((q, cap), lambda i, plan: (0, 0)),
        ),
        out_shape=jax.ShapeDtypeStruct((q, cap), jnp.bfloat16),
        compiler_params=pltpu.CompilerParams(vmem_limit_bytes=20 * 2**20),
        cost_estimate=pl.CostEstimate(
            flops=2 * q * rows * cap, bytes_accessed=2 * q * (rows + cap), transcendentals=rows
        ),
    )(jnp.stack([half, tally]).astype(jnp.int32), kept, benefit, present, behaviour, adjoint)


def dots(s_all, groups):
    cap = s_all.shape[1] // len(groups)
    value = None
    for i, group in enumerate(groups):
        blocks = [ref[...] for ref in group]
        block = blocks[0] if len(blocks) == 1 else jnp.concatenate(blocks, axis=0)
        term = jnp.dot(
            s_all[:, i * cap : (i + 1) * cap], block, preferred_element_type=jnp.float32
        )
        value = term if value is None else value + term
    return value


def near_kernel(*refs):
    s_refs, (own, e1, near, s_all) = refs[:4], refs[4:]
    q, cap = s_refs[0].shape
    for i, ref in enumerate(s_refs):
        side, other = divmod(i, 2)
        s_all[side * q : (side + 1) * q, other * cap : (other + 1) * cap] = ref[...]
    near[...] = dots(s_all, ((own,), (e1,))).astype(near.dtype)


def near_terms(s_list, own, e1):
    q, cap = s_list[0].shape
    cols = own.shape[1]
    full = pl.BlockSpec(memory_space=pltpu.VMEM)
    return pl.pallas_call(
        near_kernel,
        in_specs=[full] * 6,
        out_specs=[full] * 2,
        out_shape=[
            jax.ShapeDtypeStruct((2 * q, cols), jnp.bfloat16),
            jax.ShapeDtypeStruct((2 * q, 2 * cap), jnp.bfloat16),
        ],
        compiler_params=pltpu.CompilerParams(vmem_limit_bytes=20 * 2**20),
        cost_estimate=pl.CostEstimate(
            flops=8 * q * cap * cols, bytes_accessed=6 * 2**20, transcendentals=0
        ),
    )(*s_list, own, e1)


def terms_kernel(counts, plan, s_all, *refs):
    total, out_refs = refs[-1], refs[-5:-1]
    q = out_refs[0].shape[0]
    at = 0
    chunks = []
    for chunk in range(2):
        groups = []
        for count in counts[chunk]:
            groups.append(refs[at : at + count])
            at += count
        if len(groups) == 1:
            chunks.append(groups[0][0][...])
        else:
            chunks.append(dots(s_all, groups).astype(total.dtype))
    for chunk, value in enumerate(chunks):
        for side in range(2):
            total[2 * chunk + side] = value[side * q : (side + 1) * q]
    for slot, out_ref in enumerate(out_refs):
        out_ref[...] = total[plan[slot]]


def terms_of(plan, s_all, near, far, after=()):
    q, cols = s_all.shape[0] // 2, far[0][0].shape[1]
    groups = (*near, *far)
    counts = (tuple(len(group) for group in near), tuple(len(group) for group in far))
    values = [block for group in groups for block in group]
    full = pl.BlockSpec(memory_space=pltpu.VMEM)
    return pl.pallas_call(
        lambda *refs: terms_kernel(counts, *refs),
        in_specs=[pl.BlockSpec(memory_space=pltpu.SMEM)]
        + [full] * (1 + len(values))
        + [pl.BlockSpec(memory_space=pl.ANY)] * len(after),
        out_specs=[full] * 4,
        scratch_shapes=[pltpu.VMEM((4, q, cols), jnp.bfloat16)],
        out_shape=[jax.ShapeDtypeStruct((q, cols), jnp.bfloat16)] * 4,
        compiler_params=pltpu.CompilerParams(vmem_limit_bytes=20 * 2**20),
        cost_estimate=pl.CostEstimate(
            flops=2 * s_all.shape[0] * s_all.shape[1] * cols * len(groups) // 2,
            bytes_accessed=8 * 2**20,
            transcendentals=0,
        ),
    )(plan, s_all, *values, *after)


def rows_kernel(piece_count, plan, *refs):
    ins, outs, mine = refs[: 5 * piece_count], refs[5 * piece_count : -1], refs[-1]
    start = 0
    for piece in range(piece_count):
        *got, last, kept = ins[5 * piece : 5 * piece + 5]
        columns = slice(start, start + kept.shape[1])
        start += kept.shape[1]
        total = got[0][...].astype(jnp.float32)
        for ref in got[1:]:
            total = total + ref[...].astype(jnp.float32)

        @pl.when(plan[0] == 1)
        def _(total=total, last=last, columns=columns):
            mine[:, columns] = total + last[...].astype(jnp.float32)

        @pl.when(plan[0] == 0)
        def _(total=total, kept=kept, columns=columns):
            mine[:, columns] = total + kept[...].astype(jnp.float32)

    for step, out in enumerate(outs):
        heads, rows, head = out.shape
        at = pl.multiple_of(lax.rem(plan[1] + step, Z) * rows, 8)
        for j in range(heads):
            out[j] = mine[pl.ds(at, rows), j * head : (j + 1) * head].astype(out.dtype)


def row_blocks(plan, inputs):
    q = inputs[0].shape[0]
    cols = sum(t.shape[1] for t in inputs[::5])
    shape = (Z, q // Z, cols // Z)
    full = pl.BlockSpec(memory_space=pltpu.VMEM)
    return pl.pallas_call(
        lambda *refs: rows_kernel(len(inputs) // 5, *refs),
        in_specs=[pl.BlockSpec(memory_space=pltpu.SMEM)] + [full] * len(inputs),
        out_specs=[full] * Z,
        out_shape=[jax.ShapeDtypeStruct(shape, jnp.float32)]
        + [jax.ShapeDtypeStruct(shape, jnp.bfloat16)] * (Z - 1),
        scratch_shapes=[pltpu.VMEM((q, cols), jnp.float32)],
        compiler_params=pltpu.CompilerParams(vmem_limit_bytes=16 * 2**20),
    )(plan, *inputs)


def choose_kernel(place, *refs):
    ins, out = refs[:-1], refs[-1]
    for t in range(out.shape[0]):
        for d, ref in enumerate(ins):

            @pl.when(place[t] // Z == d)
            def _(t=t, ref=ref):
                out[t] = ref[lax.rem(place[t], Z)]


def choose(place, rows):
    full = pl.BlockSpec(memory_space=pltpu.VMEM)
    return pl.pallas_call(
        choose_kernel,
        in_specs=[pl.BlockSpec(memory_space=pltpu.SMEM)] + [full] * len(rows),
        out_specs=full,
        out_shape=jax.ShapeDtypeStruct(rows[0].shape, rows[0].dtype),
    )(place, *rows)


def polar_kernel(scale, g_ref, *refs):
    out_ref = refs[-1]
    gram = refs[0][...]
    for ref in refs[1:-1]:
        gram = gram + ref[...]

    def mul(a, b):
        return jnp.dot(a, b, precision=highest_precision_mode, preferred_element_type=jnp.float32)

    n = gram.shape[0]
    eye = (
        lax.broadcasted_iota(jnp.int32, (n, n), 0) == lax.broadcasted_iota(jnp.int32, (n, n), 1)
    ).astype(jnp.float32)
    norm = jnp.sqrt(jnp.sum(gram * eye, keepdims=True)) + norm_eps
    a1 = gram / norm / norm
    p1 = coeff_a * eye + coeff_b * a1 + coeff_c * mul(a1, a1)
    a2 = mul(mul(p1, a1), p1)
    p2 = coeff_a * eye + coeff_b * a2 + coeff_c * mul(a2, a2)
    mix = mul(p2, p1) * (scale / norm)
    out_ref[...] = mul(g_ref[...], mix).astype(out_ref.dtype)


def polar(g, grams):
    q, n = g.shape
    return pl.pallas_call(
        lambda *refs: polar_kernel(0.2 * math.sqrt(2 * DHALF), *refs),
        out_shape=jax.ShapeDtypeStruct((q, n), jnp.bfloat16),
        compiler_params=pltpu.CompilerParams(vmem_limit_bytes=16 * 2**20),
    )(g, *grams)


def on_device(
    mixer_vectors,
    upstream_adjoint,
    relative_benefit,
    present_policy_logit,
    behaviour_policy_logit,
    retained_entries,
    tallies,
    keeper_slot,
):
    bf16, f32 = jnp.bfloat16, jnp.float32
    yl, x, z = lax.axis_index("yl"), lax.axis_index("x"), lax.axis_index("z")
    yh, core = lax.axis_index("yh"), lax.axis_index("c")
    q = upstream_adjoint.shape[2]
    barrier = lax.optimization_barrier

    own = [
        pick_rows(retained_entries, mixer_vectors, start, stop)
        for start, stop in ((0, FIRST), (FIRST, mixer_vectors.shape[1]))
    ]
    adjoint = upstream_adjoint.transpose(1, 2, 0)
    kept, adjoint, own[0] = barrier((retained_entries, adjoint, own[0]))
    rows_of = [
        v[None, :] for v in (relative_benefit, present_policy_logit, behaviour_policy_logit)
    ]
    s_send = scaled_half(1 - yl, tallies[0], kept, *rows_of, adjoint)
    s_keep = scaled_half(yl, tallies[0], kept, *rows_of, adjoint)

    odd = (x + core) % 2
    near = jnp.where((x + odd) % X // 2 == yh, 0, 2)
    far = 2 - near
    plan = jnp.where(
        odd == 1,
        jnp.stack([near, far, near + 1, far + 1]),
        jnp.stack([far + 1, near + 1, far, near]),
    ).astype(jnp.int32)

    def over_x(terms):
        return [
            over_xc(terms[0], 1, 0, 2, 1),
            over_xc(terms[1], -1, 0, 0, 1),
            over_xc(terms[2], 1, 1, 2, 0),
            over_xc(terms[3], -1, 1),
            terms[3],
        ]

    e1, e3 = over_y(own[0], 1), over_y(own[0], 3)
    e1, e3, s_send, s_keep = barrier((e1, e3, s_send, s_keep))
    opposite = over_y(e1, 3)
    s_recv = over_y(s_send, 1)
    c_keep = shift(s_keep, "c", C, 1)
    s_list = (s_keep, s_recv, c_keep, shift(s_recv, "c", C, 1))
    near_product, s_all = near_terms(s_list, own[0], e1)
    opposite, near_product, second = barrier((opposite, near_product, own[1]))
    f1, f3 = over_y(second, 1), over_y(second, 3)
    first_terms = terms_of(plan, s_all, [[near_product]], [[opposite], [e3]])
    first_sums = over_x(first_terms)
    cut = second.shape[0] // 2
    fa, fb = over_y(f3[:cut], 1), over_y(f1[cut:], 3)
    second_terms = terms_of(
        plan, s_all, [[second], [f1]], [[fa, fb], [f3]], first_sums[:1]
    )
    second_sums = over_x(second_terms)

    head = mixer_vectors.shape[1] // Z
    parts = row_blocks(jnp.stack([odd, z]).astype(jnp.int32), first_sums + second_sums)
    exact = parts[0]
    for got in [shift(parts[d], "z", Z, d) for d in (4, 3, 5, 2, 6, 1, 7)]:
        exact = exact + got.astype(f32)
    rounded = exact.astype(bf16)

    heads_total = keeper_slot.shape[0]
    heads = jnp.arange(heads_total, dtype=jnp.int32)
    wanted = x * Z + jnp.arange(Z, dtype=jnp.int32)
    source = jnp.sum(
        jnp.where(keeper_slot[None, :] == wanted[:, None], heads[None, :], 0), axis=1
    )
    place = ((x - source // Z) % X * Z + source % Z).astype(jnp.int32)
    chosen = choose(place, [rounded] + [shift(rounded, "x", X, d) for d in (1, 2, 3)])
    arrived = lax.all_to_all(chosen, "z", 0, 0, tiled=True).reshape(q, head)

    g = lax.all_to_all(exact, "z", 0, 0, tiled=True).reshape(q, head)
    gram = lax.dot_general(
        g, g, (((0,), (0,)), ((), ())), precision=highest_precision_mode,
        preferred_element_type=f32,
    )
    gram = gram + shift(gram, "c", C, 1)
    update = polar(g, [gram] + [over_y(gram, flip) for flip in (2, 1, 3)])
    gradient = arrived.astype(f32).T
    return (update.T[None], gradient[None])


def solution(mesh):
    wide = Mesh(np.asarray(mesh.devices).reshape(YL, X, Z, YH, C), NAMES)
    dp, mp = ("yl", "x", "z"), ("yh", "c")
    return jax.shard_map(
        on_device,
        mesh=wide,
        in_specs=(
            P(dp, mp),
            P(dp, None, mp),
            P(dp),
            P(dp),
            P(dp),
            P(dp, None),
            P(dp),
            P(),
        ),
        out_specs=(P(dp, None, mp), P(dp, None, mp)),
        check_vma=False,
    )
```

```python
import math

import jax
import jax.numpy as jnp
import numpy as np
from jax import lax
from jax.experimental import pallas as pl
from jax.experimental.pallas import tpu as pltpu
from jax.sharding import Mesh
from jax.sharding import PartitionSpec as P

DHALF = 1792

coeff_a = 3.4445
coeff_b = -4.775
coeff_c = 2.0315
norm_eps = 1e-06
highest_precision_mode = lax.Precision.HIGHEST

YL, X, Z, YH, C = 2, 4, 8, 2, 2
NAMES = ("yl", "x", "z", "yh", "c")
FIRST = 640


def ring_pairs(flip):
    def index(y):
        return (y % 2) * 2 + y // 2

    return [(index(y), index(y ^ flip)) for y in range(4)]


def over_y(value, flip):
    return lax.ppermute(value, ("yl", "yh"), ring_pairs(flip))


def shift(value, axis, size, step):
    return lax.ppermute(value, axis, [(i, (i + step) % size) for i in range(size)])


def over_xc(value, odd_step, odd_flip, even_step=None, even_flip=0):
    pairs = []
    for x in range(X):
        for c in range(C):
            step, flip = (odd_step, odd_flip) if (x + c) % 2 else (even_step, even_flip)
            if step is not None:
                pairs.append((x * C + c, (x + step) % X * C + (c ^ flip)))
    return lax.ppermute(value, ("x", "c"), pairs)


def pick_kernel(columns, kept_ref, v_ref, out_ref):
    rows, cap = v_ref.shape[0], kept_ref.shape[1]
    column = jnp.broadcast_to(kept_ref[...], (8, cap)).T[:, :1]
    pick = lax.broadcasted_iota(jnp.int32, (cap, rows), 1) == column
    out_ref[...] = jnp.dot(
        pick.astype(jnp.bfloat16), v_ref[:, columns], preferred_element_type=jnp.float32
    ).astype(out_ref.dtype)


def pick_rows(kept, values, start, stop):
    rows = values.shape[0]
    cap = kept.shape[1]
    width = stop - start
    full = pl.BlockSpec(memory_space=pltpu.VMEM)
    return pl.pallas_call(
        lambda *refs: pick_kernel(slice(start, stop), *refs),
        in_specs=[full] * 2,
        out_specs=full,
        out_shape=jax.ShapeDtypeStruct((cap, width), values.dtype),
        compiler_params=pltpu.CompilerParams(vmem_limit_bytes=16 * 2**20),
        cost_estimate=pl.CostEstimate(
            flops=2 * cap * rows * width, bytes_accessed=2 * (rows + cap) * width, transcendentals=0
        ),
    )(kept, values)


def scale_kernel(plan, kept_ref, benefit_ref, present_ref, behaviour_ref, u_ref, out_ref):
    rows, cap = u_ref.shape[2], kept_ref.shape[1]
    pick = (lax.broadcasted_iota(jnp.int32, (rows, cap), 0) == kept_ref[...]).astype(jnp.bfloat16)
    rest = benefit_ref[...] * jnp.exp(present_ref[...] - behaviour_ref[...])
    parts = []
    for _ in range(3):
        part = rest.astype(jnp.bfloat16)
        parts.append(part)
        rest = rest - part.astype(jnp.float32)
    weight = jnp.zeros((1, cap), jnp.float32)
    for part in parts[::-1]:
        stacked = jnp.broadcast_to(part, (16, rows))
        weight = weight + jnp.dot(stacked, pick, preferred_element_type=jnp.float32)[:1]
    live = lax.broadcasted_iota(jnp.int32, (1, cap), 1) < plan[1]
    weight = jnp.where(live, weight, 0.0)
    picked = jnp.dot(u_ref[0], pick, preferred_element_type=jnp.float32)
    out_ref[...] = (weight * picked).astype(out_ref.dtype)


def scaled_half(half, tally, kept, benefit, present, behaviour, adjoint):
    _, q, rows = adjoint.shape
    cap = kept.shape[1]
    row_spec = pl.BlockSpec((1, rows), lambda i, plan: (0, 0))
    return pl.pallas_call(
        scale_kernel,
        grid_spec=pltpu.PrefetchScalarGridSpec(
            num_scalar_prefetch=1,
            grid=(1,),
            in_specs=[
                pl.BlockSpec((1, cap), lambda i, plan: (0, 0)),
                row_spec,
                row_spec,
                row_spec,
                pl.BlockSpec((1, q, rows), lambda i, plan: (plan[0], 0, 0)),
            ],
            out_specs=pl.BlockSpec((q, cap), lambda i, plan: (0, 0)),
        ),
        out_shape=jax.ShapeDtypeStruct((q, cap), jnp.bfloat16),
        compiler_params=pltpu.CompilerParams(vmem_limit_bytes=20 * 2**20),
        cost_estimate=pl.CostEstimate(
            flops=2 * q * rows * cap, bytes_accessed=2 * q * (rows + cap), transcendentals=rows
        ),
    )(jnp.stack([half, tally]).astype(jnp.int32), kept, benefit, present, behaviour, adjoint)


def dots(s_all, groups):
    cap = s_all.shape[1] // len(groups)
    value = None
    for i, group in enumerate(groups):
        blocks = [ref[...] for ref in group]
        block = blocks[0] if len(blocks) == 1 else jnp.concatenate(blocks, axis=0)
        term = jnp.dot(
            s_all[:, i * cap : (i + 1) * cap], block, preferred_element_type=jnp.float32
        )
        value = term if value is None else value + term
    return value


def near_kernel(*refs):
    s_refs, (own, e1, near, s_all) = refs[:4], refs[4:]
    q, cap = s_refs[0].shape
    for i, ref in enumerate(s_refs):
        side, other = divmod(i, 2)
        s_all[side * q : (side + 1) * q, other * cap : (other + 1) * cap] = ref[...]
    near[...] = dots(s_all, ((own,), (e1,))).astype(near.dtype)


def near_terms(s_list, own, e1):
    q, cap = s_list[0].shape
    cols = own.shape[1]
    full = pl.BlockSpec(memory_space=pltpu.VMEM)
    return pl.pallas_call(
        near_kernel,
        in_specs=[full] * 6,
        out_specs=[full] * 2,
        out_shape=[
            jax.ShapeDtypeStruct((2 * q, cols), jnp.bfloat16),
            jax.ShapeDtypeStruct((2 * q, 2 * cap), jnp.bfloat16),
        ],
        compiler_params=pltpu.CompilerParams(vmem_limit_bytes=20 * 2**20),
        cost_estimate=pl.CostEstimate(
            flops=8 * q * cap * cols, bytes_accessed=6 * 2**20, transcendentals=0
        ),
    )(*s_list, own, e1)


def terms_kernel(counts, plan, s_all, *refs):
    total, out_refs = refs[-1], refs[-5:-1]
    q = out_refs[0].shape[0]
    at = 0
    chunks = []
    for chunk in range(2):
        groups = []
        for count in counts[chunk]:
            groups.append(refs[at : at + count])
            at += count
        if len(groups) == 1:
            chunks.append(groups[0][0][...])
        else:
            chunks.append(dots(s_all, groups).astype(total.dtype))
    for chunk, value in enumerate(chunks):
        for side in range(2):
            total[2 * chunk + side] = value[side * q : (side + 1) * q]
    for slot, out_ref in enumerate(out_refs):
        out_ref[...] = total[plan[slot]]


def terms_of(plan, s_all, near, far, after=()):
    q, cols = s_all.shape[0] // 2, far[0][0].shape[1]
    groups = (*near, *far)
    counts = (tuple(len(group) for group in near), tuple(len(group) for group in far))
    values = [block for group in groups for block in group]
    full = pl.BlockSpec(memory_space=pltpu.VMEM)
    return pl.pallas_call(
        lambda *refs: terms_kernel(counts, *refs),
        in_specs=[pl.BlockSpec(memory_space=pltpu.SMEM)]
        + [full] * (1 + len(values))
        + [pl.BlockSpec(memory_space=pl.ANY)] * len(after),
        out_specs=[full] * 4,
        scratch_shapes=[pltpu.VMEM((4, q, cols), jnp.bfloat16)],
        out_shape=[jax.ShapeDtypeStruct((q, cols), jnp.bfloat16)] * 4,
        compiler_params=pltpu.CompilerParams(vmem_limit_bytes=20 * 2**20),
        cost_estimate=pl.CostEstimate(
            flops=2 * s_all.shape[0] * s_all.shape[1] * cols * len(groups) // 2,
            bytes_accessed=8 * 2**20,
            transcendentals=0,
        ),
    )(plan, s_all, *values, *after)


def rows_kernel(piece_count, plan, *refs):
    ins, outs, mine = refs[: 5 * piece_count], refs[5 * piece_count : -1], refs[-1]
    start = 0
    for piece in range(piece_count):
        *got, last, kept = ins[5 * piece : 5 * piece + 5]
        columns = slice(start, start + kept.shape[1])
        start += kept.shape[1]
        total = got[0][...].astype(jnp.float32)
        for ref in got[1:]:
            total = total + ref[...].astype(jnp.float32)

        @pl.when(plan[0] == 1)
        def _(total=total, last=last, columns=columns):
            mine[:, columns] = total + last[...].astype(jnp.float32)

        @pl.when(plan[0] == 0)
        def _(total=total, kept=kept, columns=columns):
            mine[:, columns] = total + kept[...].astype(jnp.float32)

    for step, out in enumerate(outs):
        heads, rows, head = out.shape
        at = pl.multiple_of(lax.rem(plan[1] + step, Z) * rows, 8)
        for j in range(heads):
            out[j] = mine[pl.ds(at, rows), j * head : (j + 1) * head].astype(out.dtype)


def row_blocks(plan, inputs, head):
    q = inputs[0].shape[0]
    cols = sum(t.shape[1] for t in inputs[::5])
    shape = (cols // head, q // Z, head)
    full = pl.BlockSpec(memory_space=pltpu.VMEM)
    return pl.pallas_call(
        lambda *refs: rows_kernel(len(inputs) // 5, *refs),
        in_specs=[pl.BlockSpec(memory_space=pltpu.SMEM)] + [full] * len(inputs),
        out_specs=[full] * Z,
        out_shape=[jax.ShapeDtypeStruct(shape, jnp.float32)]
        + [jax.ShapeDtypeStruct(shape, jnp.bfloat16)] * (Z - 1),
        scratch_shapes=[pltpu.VMEM((q, cols), jnp.float32)],
        compiler_params=pltpu.CompilerParams(vmem_limit_bytes=16 * 2**20),
    )(plan, *inputs)


def choose_kernel(place, *refs):
    ins, out = refs[:-1], refs[-1]
    for t in range(out.shape[0]):
        for d, ref in enumerate(ins):

            @pl.when(place[t] // Z == d)
            def _(t=t, ref=ref):
                out[t] = ref[lax.rem(place[t], Z)]


def choose(place, rows):
    full = pl.BlockSpec(memory_space=pltpu.VMEM)
    return pl.pallas_call(
        choose_kernel,
        in_specs=[pl.BlockSpec(memory_space=pltpu.SMEM)] + [full] * len(rows),
        out_specs=full,
        out_shape=jax.ShapeDtypeStruct(rows[0].shape, rows[0].dtype),
    )(place, *rows)


def polar_kernel(scale, g_ref, *refs):
    out_ref = refs[-1]
    gram = refs[0][...]
    for ref in refs[1:-1]:
        gram = gram + ref[...]

    def mul(a, b):
        return jnp.dot(a, b, precision=highest_precision_mode, preferred_element_type=jnp.float32)

    n = gram.shape[0]
    eye = (
        lax.broadcasted_iota(jnp.int32, (n, n), 0) == lax.broadcasted_iota(jnp.int32, (n, n), 1)
    ).astype(jnp.float32)
    norm = jnp.sqrt(jnp.sum(gram * eye, keepdims=True)) + norm_eps
    a1 = gram / norm / norm
    p1 = coeff_a * eye + coeff_b * a1 + coeff_c * mul(a1, a1)
    a2 = mul(mul(p1, a1), p1)
    p2 = coeff_a * eye + coeff_b * a2 + coeff_c * mul(a2, a2)
    mix = mul(p2, p1) * (scale / norm)
    out_ref[...] = mul(g_ref[...], mix).astype(out_ref.dtype)


def polar(g, grams):
    q, n = g.shape
    return pl.pallas_call(
        lambda *refs: polar_kernel(0.2 * math.sqrt(2 * DHALF), *refs),
        out_shape=jax.ShapeDtypeStruct((q, n), jnp.bfloat16),
        compiler_params=pltpu.CompilerParams(vmem_limit_bytes=16 * 2**20),
    )(g, *grams)


def on_device(
    mixer_vectors,
    upstream_adjoint,
    relative_benefit,
    present_policy_logit,
    behaviour_policy_logit,
    retained_entries,
    tallies,
    keeper_slot,
):
    bf16, f32 = jnp.bfloat16, jnp.float32
    yl, x, z = lax.axis_index("yl"), lax.axis_index("x"), lax.axis_index("z")
    yh, core = lax.axis_index("yh"), lax.axis_index("c")
    q = upstream_adjoint.shape[2]
    barrier = lax.optimization_barrier

    own = [
        pick_rows(retained_entries, mixer_vectors, start, stop)
        for start, stop in ((0, FIRST), (FIRST, mixer_vectors.shape[1]))
    ]
    adjoint = upstream_adjoint.transpose(1, 2, 0)
    kept, adjoint, own[0] = barrier((retained_entries, adjoint, own[0]))
    rows_of = [
        v[None, :] for v in (relative_benefit, present_policy_logit, behaviour_policy_logit)
    ]
    s_send = scaled_half(1 - yl, tallies[0], kept, *rows_of, adjoint)
    s_keep = scaled_half(yl, tallies[0], kept, *rows_of, adjoint)

    odd = (x + core) % 2
    near = jnp.where((x + odd) % X // 2 == yh, 0, 2)
    far = 2 - near
    plan = jnp.where(
        odd == 1,
        jnp.stack([near, far, near + 1, far + 1]),
        jnp.stack([far + 1, near + 1, far, near]),
    ).astype(jnp.int32)

    def over_x(terms):
        return [
            over_xc(terms[0], 1, 0, 2, 1),
            over_xc(terms[1], -1, 0, 0, 1),
            over_xc(terms[2], 1, 1, 2, 0),
            over_xc(terms[3], -1, 1),
            terms[3],
        ]

    e1, e3 = over_y(own[0], 1), over_y(own[0], 3)
    e1, e3, s_send, s_keep = barrier((e1, e3, s_send, s_keep))
    opposite = over_y(e1, 3)
    s_recv = over_y(s_send, 1)
    c_keep = shift(s_keep, "c", C, 1)
    s_list = (s_keep, s_recv, c_keep, shift(s_recv, "c", C, 1))
    near_product, s_all = near_terms(s_list, own[0], e1)
    opposite, near_product, second = barrier((opposite, near_product, own[1]))
    f1, f3 = over_y(second, 1), over_y(second, 3)
    first_terms = terms_of(plan, s_all, [[near_product]], [[opposite], [e3]])
    first_sums = over_x(first_terms)
    cut = second.shape[0] // 2
    fa, fb = over_y(f3[:cut], 1), over_y(f1[cut:], 3)
    second_terms = terms_of(
        plan, s_all, [[second], [f1]], [[fa, fb], [f3]], first_sums[:1]
    )
    second_sums = over_x(second_terms)

    head = mixer_vectors.shape[1] // Z
    where = jnp.stack([odd, z]).astype(jnp.int32)
    exact = []
    for sums in (first_sums, second_sums):
        parts = row_blocks(where, sums, head)
        total = parts[0]
        for got in [shift(parts[d], "z", Z, d) for d in (4, 3, 5, 2, 6, 1, 7)]:
            total = total + got.astype(f32)
        exact.append(total)
    exact = jnp.concatenate(exact)
    rounded = exact.astype(bf16)

    heads_total = keeper_slot.shape[0]
    heads = jnp.arange(heads_total, dtype=jnp.int32)
    wanted = x * Z + jnp.arange(Z, dtype=jnp.int32)
    source = jnp.sum(
        jnp.where(keeper_slot[None, :] == wanted[:, None], heads[None, :], 0), axis=1
    )
    place = ((x - source // Z) % X * Z + source % Z).astype(jnp.int32)
    chosen = choose(place, [rounded] + [shift(rounded, "x", X, d) for d in (1, 2, 3)])
    arrived = lax.all_to_all(chosen, "z", 0, 0, tiled=True).reshape(q, head)

    g = lax.all_to_all(exact, "z", 0, 0, tiled=True).reshape(q, head)
    gram = lax.dot_general(
        g, g, (((0,), (0,)), ((), ())), precision=highest_precision_mode,
        preferred_element_type=f32,
    )
    gram = gram + shift(gram, "c", C, 1)
    update = polar(g, [gram] + [over_y(gram, flip) for flip in (2, 1, 3)])
    gradient = arrived.astype(f32).T
    return (update.T[None], gradient[None])


def solution(mesh):
    wide = Mesh(np.asarray(mesh.devices).reshape(YL, X, Z, YH, C), NAMES)
    dp, mp = ("yl", "x", "z"), ("yh", "c")
    return jax.shard_map(
        on_device,
        mesh=wide,
        in_specs=(
            P(dp, mp),
            P(dp, None, mp),
            P(dp),
            P(dp),
            P(dp),
            P(dp, None),
            P(dp),
            P(),
        ),
        out_specs=(P(dp, None, mp), P(dp, None, mp)),
        check_vma=False,
    )
```

```python
import math

import jax
import jax.numpy as jnp
import numpy as np
from jax import lax
from jax.experimental import pallas as pl
from jax.experimental.pallas import tpu as pltpu
from jax.sharding import Mesh
from jax.sharding import PartitionSpec as P

DHALF = 1792

coeff_a = 3.4445
coeff_b = -4.775
coeff_c = 2.0315
norm_eps = 1e-06
highest_precision_mode = lax.Precision.HIGHEST

YL, X, Z, YH, C = 2, 4, 8, 2, 2
NAMES = ("yl", "x", "z", "yh", "c")
FIRST = 640


def ring_pairs(flip):
    def index(y):
        return (y % 2) * 2 + y // 2

    return [(index(y), index(y ^ flip)) for y in range(4)]


def over_y(value, flip):
    return lax.ppermute(value, ("yl", "yh"), ring_pairs(flip))


def shift(value, axis, size, step):
    return lax.ppermute(value, axis, [(i, (i + step) % size) for i in range(size)])


def over_xc(value, odd_step, odd_flip, even_step=None, even_flip=0):
    pairs = []
    for x in range(X):
        for c in range(C):
            step, flip = (odd_step, odd_flip) if (x + c) % 2 else (even_step, even_flip)
            if step is not None:
                pairs.append((x * C + c, (x + step) % X * C + (c ^ flip)))
    return lax.ppermute(value, ("x", "c"), pairs)


def pick_kernel(columns, kept_ref, v_ref, out_ref):
    rows, cap = v_ref.shape[0], kept_ref.shape[1]
    column = jnp.broadcast_to(kept_ref[...], (8, cap)).T[:, :1]
    pick = lax.broadcasted_iota(jnp.int32, (cap, rows), 1) == column
    out_ref[...] = jnp.dot(
        pick.astype(jnp.bfloat16), v_ref[:, columns], preferred_element_type=jnp.float32
    ).astype(out_ref.dtype)


def pick_rows(kept, values, start, stop):
    rows = values.shape[0]
    cap = kept.shape[1]
    width = stop - start
    full = pl.BlockSpec(memory_space=pltpu.VMEM)
    return pl.pallas_call(
        lambda *refs: pick_kernel(slice(start, stop), *refs),
        in_specs=[full] * 2,
        out_specs=full,
        out_shape=jax.ShapeDtypeStruct((cap, width), values.dtype),
        compiler_params=pltpu.CompilerParams(vmem_limit_bytes=16 * 2**20),
        cost_estimate=pl.CostEstimate(
            flops=2 * cap * rows * width, bytes_accessed=2 * (rows + cap) * width, transcendentals=0
        ),
    )(kept, values)


def scale_kernel(plan, kept_ref, benefit_ref, present_ref, behaviour_ref, u_ref, out_ref):
    rows, cap = u_ref.shape[2], kept_ref.shape[1]
    pick = (lax.broadcasted_iota(jnp.int32, (rows, cap), 0) == kept_ref[...]).astype(jnp.bfloat16)
    rest = benefit_ref[...] * jnp.exp(present_ref[...] - behaviour_ref[...])
    parts = []
    for _ in range(3):
        part = rest.astype(jnp.bfloat16)
        parts.append(part)
        rest = rest - part.astype(jnp.float32)
    weight = jnp.zeros((1, cap), jnp.float32)
    for part in parts[::-1]:
        stacked = jnp.broadcast_to(part, (16, rows))
        weight = weight + jnp.dot(stacked, pick, preferred_element_type=jnp.float32)[:1]
    live = lax.broadcasted_iota(jnp.int32, (1, cap), 1) < plan[1]
    weight = jnp.where(live, weight, 0.0)
    picked = jnp.dot(u_ref[0], pick, preferred_element_type=jnp.float32)
    out_ref[...] = (weight * picked).astype(out_ref.dtype)


def scaled_half(half, tally, kept, benefit, present, behaviour, adjoint):
    _, q, rows = adjoint.shape
    cap = kept.shape[1]
    row_spec = pl.BlockSpec((1, rows), lambda i, plan: (0, 0))
    return pl.pallas_call(
        scale_kernel,
        grid_spec=pltpu.PrefetchScalarGridSpec(
            num_scalar_prefetch=1,
            grid=(1,),
            in_specs=[
                pl.BlockSpec((1, cap), lambda i, plan: (0, 0)),
                row_spec,
                row_spec,
                row_spec,
                pl.BlockSpec((1, q, rows), lambda i, plan: (plan[0], 0, 0)),
            ],
            out_specs=pl.BlockSpec((q, cap), lambda i, plan: (0, 0)),
        ),
        out_shape=jax.ShapeDtypeStruct((q, cap), jnp.bfloat16),
        compiler_params=pltpu.CompilerParams(vmem_limit_bytes=20 * 2**20),
        cost_estimate=pl.CostEstimate(
            flops=2 * q * rows * cap, bytes_accessed=2 * q * (rows + cap), transcendentals=rows
        ),
    )(jnp.stack([half, tally]).astype(jnp.int32), kept, benefit, present, behaviour, adjoint)


def slots_of():
    x, core, yh = lax.axis_index("x"), lax.axis_index("c"), lax.axis_index("yh")
    odd = lax.rem(x + core, 2)
    near = jnp.where(lax.div(lax.rem(x + odd, X), 2) == yh, 0, 2)
    far = 2 - near
    odd_slots = (near, far, near + 1, far + 1)
    even_slots = (far + 1, near + 1, far, near)
    return [jnp.where(odd == 1, a, b) for a, b in zip(odd_slots, even_slots)]


def dots(s_all, groups):
    cap = s_all.shape[1] // len(groups)
    value = None
    for i, group in enumerate(groups):
        blocks = [ref[...] for ref in group]
        block = blocks[0] if len(blocks) == 1 else jnp.concatenate(blocks, axis=0)
        term = jnp.dot(
            s_all[:, i * cap : (i + 1) * cap], block, preferred_element_type=jnp.float32
        )
        value = term if value is None else value + term
    return value


def near_kernel(*refs):
    s_refs, (own, e1, near, s_all) = refs[:4], refs[4:]
    q, cap = s_refs[0].shape
    for i, ref in enumerate(s_refs):
        side, other = divmod(i, 2)
        s_all[side * q : (side + 1) * q, other * cap : (other + 1) * cap] = ref[...]
    near[...] = dots(s_all, ((own,), (e1,))).astype(near.dtype)


def near_terms(s_list, own, e1):
    q, cap = s_list[0].shape
    cols = own.shape[1]
    full = pl.BlockSpec(memory_space=pltpu.VMEM)
    return pl.pallas_call(
        near_kernel,
        in_specs=[full] * 6,
        out_specs=[full] * 2,
        out_shape=[
            jax.ShapeDtypeStruct((2 * q, cols), jnp.bfloat16),
            jax.ShapeDtypeStruct((2 * q, 2 * cap), jnp.bfloat16),
        ],
        compiler_params=pltpu.CompilerParams(vmem_limit_bytes=20 * 2**20),
        cost_estimate=pl.CostEstimate(
            flops=8 * q * cap * cols, bytes_accessed=6 * 2**20, transcendentals=0
        ),
    )(*s_list, own, e1)


def terms_kernel(counts, s_all, *refs):
    total, out_refs = refs[-1], refs[-5:-1]
    q = out_refs[0].shape[0]
    at = 0
    chunks = []
    for chunk in range(2):
        groups = []
        for count in counts[chunk]:
            groups.append(refs[at : at + count])
            at += count
        if len(groups) == 1:
            chunks.append(groups[0][0][...])
        else:
            chunks.append(dots(s_all, groups).astype(total.dtype))
    for chunk, value in enumerate(chunks):
        for side in range(2):
            total[2 * chunk + side] = value[side * q : (side + 1) * q]
    for slot, out_ref in zip(slots_of(), out_refs):
        out_ref[...] = total[slot]


def terms_of(s_all, near, far, after=()):
    q, cols = s_all.shape[0] // 2, far[0][0].shape[1]
    groups = (*near, *far)
    counts = (tuple(len(group) for group in near), tuple(len(group) for group in far))
    values = [block for group in groups for block in group]
    full = pl.BlockSpec(memory_space=pltpu.VMEM)
    return pl.pallas_call(
        lambda *refs: terms_kernel(counts, *refs),
        in_specs=[full] * (1 + len(values))
        + [pl.BlockSpec(memory_space=pl.ANY)] * len(after),
        out_specs=[full] * 4,
        scratch_shapes=[pltpu.VMEM((4, q, cols), jnp.bfloat16)],
        out_shape=[jax.ShapeDtypeStruct((q, cols), jnp.bfloat16)] * 4,
        compiler_params=pltpu.CompilerParams(vmem_limit_bytes=20 * 2**20),
        cost_estimate=pl.CostEstimate(
            flops=2 * s_all.shape[0] * s_all.shape[1] * cols * len(groups) // 2,
            bytes_accessed=8 * 2**20,
            transcendentals=0,
        ),
    )(s_all, *values, *after)


def rows_kernel(piece_count, *refs):
    odd = lax.rem(lax.axis_index("x") + lax.axis_index("c"), 2)
    z = lax.axis_index("z")
    ins, outs, mine = refs[: 5 * piece_count], refs[5 * piece_count : -1], refs[-1]
    start = 0
    for piece in range(piece_count):
        *got, last, kept = ins[5 * piece : 5 * piece + 5]
        columns = slice(start, start + kept.shape[1])
        start += kept.shape[1]
        total = got[0][...].astype(jnp.float32)
        for ref in got[1:]:
            total = total + ref[...].astype(jnp.float32)

        @pl.when(odd == 1)
        def _(total=total, last=last, columns=columns):
            mine[:, columns] = total + last[...].astype(jnp.float32)

        @pl.when(odd == 0)
        def _(total=total, kept=kept, columns=columns):
            mine[:, columns] = total + kept[...].astype(jnp.float32)

    for step, out in enumerate(outs):
        heads, rows, head = out.shape
        at = pl.multiple_of(lax.rem(z + step, Z) * rows, 8)
        for j in range(heads):
            out[j] = mine[pl.ds(at, rows), j * head : (j + 1) * head].astype(out.dtype)


def row_blocks(inputs):
    q = inputs[0].shape[0]
    cols = sum(t.shape[1] for t in inputs[::5])
    shape = (Z, q // Z, cols // Z)
    full = pl.BlockSpec(memory_space=pltpu.VMEM)
    return pl.pallas_call(
        lambda *refs: rows_kernel(len(inputs) // 5, *refs),
        in_specs=[full] * len(inputs),
        out_specs=[full] * Z,
        out_shape=[jax.ShapeDtypeStruct(shape, jnp.float32)]
        + [jax.ShapeDtypeStruct(shape, jnp.bfloat16)] * (Z - 1),
        scratch_shapes=[pltpu.VMEM((q, cols), jnp.float32)],
        compiler_params=pltpu.CompilerParams(vmem_limit_bytes=16 * 2**20),
    )(*inputs)


def choose_kernel(place, *refs):
    ins, out = refs[:-1], refs[-1]
    for t in range(out.shape[0]):
        for d, ref in enumerate(ins):

            @pl.when(place[t] // Z == d)
            def _(t=t, ref=ref):
                out[t] = ref[lax.rem(place[t], Z)]


def choose(place, rows):
    full = pl.BlockSpec(memory_space=pltpu.VMEM)
    return pl.pallas_call(
        choose_kernel,
        in_specs=[pl.BlockSpec(memory_space=pltpu.SMEM)] + [full] * len(rows),
        out_specs=full,
        out_shape=jax.ShapeDtypeStruct(rows[0].shape, rows[0].dtype),
    )(place, *rows)


def polar_kernel(scale, g_ref, *refs):
    out_ref = refs[-1]
    gram = refs[0][...]
    for ref in refs[1:-1]:
        gram = gram + ref[...]

    def mul(a, b):
        return jnp.dot(a, b, precision=highest_precision_mode, preferred_element_type=jnp.float32)

    n = gram.shape[0]
    eye = (
        lax.broadcasted_iota(jnp.int32, (n, n), 0) == lax.broadcasted_iota(jnp.int32, (n, n), 1)
    ).astype(jnp.float32)
    norm = jnp.sqrt(jnp.sum(gram * eye, keepdims=True)) + norm_eps
    a1 = gram / norm / norm
    p1 = coeff_a * eye + coeff_b * a1 + coeff_c * mul(a1, a1)
    a2 = mul(mul(p1, a1), p1)
    p2 = coeff_a * eye + coeff_b * a2 + coeff_c * mul(a2, a2)
    mix = mul(p2, p1) * (scale / norm)
    out_ref[...] = mul(g_ref[...], mix).astype(out_ref.dtype)


def polar(g, grams):
    q, n = g.shape
    return pl.pallas_call(
        lambda *refs: polar_kernel(0.2 * math.sqrt(2 * DHALF), *refs),
        out_shape=jax.ShapeDtypeStruct((q, n), jnp.bfloat16),
        compiler_params=pltpu.CompilerParams(vmem_limit_bytes=16 * 2**20),
    )(g, *grams)


def on_device(
    mixer_vectors,
    upstream_adjoint,
    relative_benefit,
    present_policy_logit,
    behaviour_policy_logit,
    retained_entries,
    tallies,
    keeper_slot,
):
    bf16, f32 = jnp.bfloat16, jnp.float32
    yl, x, z = lax.axis_index("yl"), lax.axis_index("x"), lax.axis_index("z")
    yh, core = lax.axis_index("yh"), lax.axis_index("c")
    q = upstream_adjoint.shape[2]
    barrier = lax.optimization_barrier

    own = [
        pick_rows(retained_entries, mixer_vectors, start, stop)
        for start, stop in ((0, FIRST), (FIRST, mixer_vectors.shape[1]))
    ]
    adjoint = upstream_adjoint.transpose(1, 2, 0)
    kept, adjoint, own[0] = barrier((retained_entries, adjoint, own[0]))
    rows_of = [
        v[None, :] for v in (relative_benefit, present_policy_logit, behaviour_policy_logit)
    ]
    s_send = scaled_half(1 - yl, tallies[0], kept, *rows_of, adjoint)
    s_keep = scaled_half(yl, tallies[0], kept, *rows_of, adjoint)

    def over_x(terms):
        return [
            over_xc(terms[0], 1, 0, 2, 1),
            over_xc(terms[1], -1, 0, 0, 1),
            over_xc(terms[2], 1, 1, 2, 0),
            over_xc(terms[3], -1, 1),
            terms[3],
        ]

    e1, e3 = over_y(own[0], 1), over_y(own[0], 3)
    e1, e3, s_send, s_keep = barrier((e1, e3, s_send, s_keep))
    opposite = over_y(e1, 3)
    s_recv = over_y(s_send, 1)
    c_keep = shift(s_keep, "c", C, 1)
    s_list = (s_keep, s_recv, c_keep, shift(s_recv, "c", C, 1))
    near_product, s_all = near_terms(s_list, own[0], e1)
    opposite, near_product, second = barrier((opposite, near_product, own[1]))
    f1, f3 = over_y(second, 1), over_y(second, 3)
    first_terms = terms_of(s_all, [[near_product]], [[opposite], [e3]])
    first_sums = over_x(first_terms)
    cut = second.shape[0] // 2
    fa, fb = over_y(f3[:cut], 1), over_y(f1[cut:], 3)
    second_terms = terms_of(
        s_all, [[second], [f1]], [[fa, fb], [f3]], first_sums[:1]
    )
    second_sums = over_x(second_terms)

    head = mixer_vectors.shape[1] // Z
    parts = row_blocks(first_sums + second_sums)
    exact = parts[0]
    for got in [shift(parts[d], "z", Z, d) for d in (4, 3, 5, 2, 6, 1, 7)]:
        exact = exact + got.astype(f32)
    rounded = exact.astype(bf16)

    heads_total = keeper_slot.shape[0]
    heads = jnp.arange(heads_total, dtype=jnp.int32)
    wanted = x * Z + jnp.arange(Z, dtype=jnp.int32)
    source = jnp.sum(
        jnp.where(keeper_slot[None, :] == wanted[:, None], heads[None, :], 0), axis=1
    )
    place = ((x - source // Z) % X * Z + source % Z).astype(jnp.int32)
    chosen = choose(place, [rounded] + [shift(rounded, "x", X, d) for d in (1, 2, 3)])
    arrived = lax.all_to_all(chosen, "z", 0, 0, tiled=True).reshape(q, head)

    g = lax.all_to_all(exact, "z", 0, 0, tiled=True).reshape(q, head)
    gram = lax.dot_general(
        g, g, (((0,), (0,)), ((), ())), precision=highest_precision_mode,
        preferred_element_type=f32,
    )
    gram = gram + shift(gram, "c", C, 1)
    update = polar(g, [gram] + [over_y(gram, flip) for flip in (2, 1, 3)])
    gradient = arrived.astype(f32).T
    return (update.T[None], gradient[None])


def solution(mesh):
    wide = Mesh(np.asarray(mesh.devices).reshape(YL, X, Z, YH, C), NAMES)
    dp, mp = ("yl", "x", "z"), ("yh", "c")
    return jax.shard_map(
        on_device,
        mesh=wide,
        in_specs=(
            P(dp, mp),
            P(dp, None, mp),
            P(dp),
            P(dp),
            P(dp),
            P(dp, None),
            P(dp),
            P(),
        ),
        out_specs=(P(dp, None, mp), P(dp, None, mp)),
        check_vma=False,
    )
```
